128 devices in a mesh: dp: 16 (over z, x), ctx: 8 (over y, core).
Axes of the slice: x: 4, y: 4, z: 4, core: 2. Of those that a mesh axis runs over, the one named last changes fastest.
Arguments:
- grad_query: bfloat16 [128, 1536, 6144], P(('dp', 'ctx')), may hold values from -6 to 6
- grad_key: bfloat16 [128, 512, 4096], P(('dp', 'ctx')), may hold values from -6 to 6
- query_weight: float32 [1536, 6144], P('ctx', 'dp'), may hold values from -1.25 to 1.25
- key_weight: float32 [512, 4096], P('ctx', 'dp'), may hold values from -1.25 to 1.25
- query_moment: float32 [1536, 6144], P('ctx', 'dp'), may hold values from -6 to 6
- key_moment: float32 [512, 4096], P('ctx', 'dp'), may hold values from -6 to 6
- max_logits: float32 [128, 32], P(('dp', 'ctx')), may hold values from 20 to 300, as said below
Outputs:
- new_query_weight: bfloat16 [1536, 6144], P('ctx')
- new_key_weight: bfloat16 [512, 4096], P('ctx')
- new_query_moment: float32 [1536, 6144], P('ctx', 'dp')
- new_key_moment: float32 [512, 4096], P('ctx', 'dp')
The draws below stay inside these ranges and needn't reach their ends.
Inputs may be any that keep to these rules, and one draw needn't show every extreme that they name: `max_logits`: for every head one device holds a value clearly larger than all the others of that head.
All inputs are finite; a program needn't handle non-finite values.
Results may differ from the reference program's by a relative error of at most 0.014.
Values may be sent and summed in bfloat16 or wider, within the bound.
No kernel may reach another device: no remote copies, remote signals or barrier semaphores. Data moves between devices by JAX's collectives and lax.ppermute only.
A program may use at most 128 MiB of HBM per device.

```python
import math
import jax
import jax.numpy as jnp
from jax import lax

HEADS = 32
QL = 1536
KVL = 512
QH = 192
QROPE = 64
KH = 128
ITERS = 5
N_DP = 16
N_CTX = 8


def draw_max_logits(key, part):
    key = jax.random.fold_in(key, 7)
    first_key, second_key, third_key = jax.random.split(key, 3)
    devices = N_DP * N_CTX
    base = jax.random.uniform(first_key, (devices, HEADS), jnp.float32, 20.0, 60.0)
    winner = jax.random.randint(second_key, (HEADS,), 0, devices)
    peak = jax.random.uniform(third_key, (HEADS,), jnp.float32, 65.0, 300.0)
    device_rows = lax.broadcasted_iota(jnp.int32, (devices, HEADS), 0)
    return jnp.where(device_rows == winner[None, :], peak[None, :], base)


def raised(entries, own_key, source, target, parts, factor):
    def block_of(axis_at):
        return (jnp.arange(entries.shape[axis_at]) // (entries.shape[axis_at] // parts)).reshape((-1,) + (1,) * (entries.ndim - 1 - axis_at))

    one_side = jax.random.permutation(own_key, parts)[block_of(target)]
    second = (block_of(target) + parts // 2) % parts
    return jnp.where((block_of(source) == one_side) | (block_of(source) == second), factor * entries, entries)


def block_levels(own_key, shape, shards, low, largest):
    def one(dim, parts):
        steps = jax.random.uniform(jax.random.fold_in(jax.random.fold_in(own_key, 6), dim), (parts,), jnp.float32, low / len(shards), largest / len(shards))
        return jnp.repeat(jnp.exp(steps), shape[dim] // parts).reshape((-1,) + (1,) * (len(shape) - dim - 1))

    gain = one(*shards[0])
    for cut in shards[1:]:
        gain = gain * one(*cut)
    return gain


def noise(stream_key, shape, spread, most, cuts=(), dtype=jnp.bfloat16):
    level = block_levels(stream_key, shape, cuts, -0.22, 0.18) if cuts else 1.0
    drawn = jax.random.normal(stream_key, shape, jnp.float32) * spread * level
    return jnp.minimum(jnp.maximum(drawn, -most), most).astype(dtype)


def heavy_noise(rng, shape, scale, most, cuts, heavy, held_as=jnp.bfloat16):
    drawn = scale * jax.random.normal(rng, shape, jnp.float32)
    if cuts:
        drawn = drawn * block_levels(rng, shape, cuts, -0.22, 0.18)
    return jnp.clip(raised(drawn, jax.random.fold_in(rng, 3), *heavy), -most, most).astype(held_as)


def setup_inputs(seed: int = 0) -> dict:
    splits = jax.random.split(jax.random.key(seed), 8)
    grad_query = heavy_noise(splits[0], (N_DP * N_CTX, QL, HEADS * QH), 0.1, 6.0, ((0, 128),), (0, 2, 128, 5.5))
    grad_key = heavy_noise(splits[1], (N_DP * N_CTX, KVL, HEADS * KH), 0.1, 6.0, ((0, 128),), (0, 2, 128, 5.5))
    query_weight = noise(splits[2], (QL, HEADS * QH), 0.08, 1.25, ((0, 8), (1, 16)), jnp.float32)
    key_weight = noise(splits[3], (KVL, HEADS * KH), 0.08, 1.25, ((0, 8), (1, 16)), jnp.float32)
    query_moment = noise(splits[4], (QL, HEADS * QH), 1.0, 6.0, ((0, 8), (1, 16)), jnp.float32)
    key_moment = noise(splits[5], (KVL, HEADS * KH), 1.0, 6.0, ((0, 8), (1, 16)), jnp.float32)
    max_logits = draw_max_logits(jax.random.fold_in(splits[7], 71), 0)
    return dict(grad_query=grad_query, grad_key=grad_key, query_weight=query_weight, key_weight=key_weight, query_moment=query_moment, key_moment=key_moment, max_logits=max_logits)


momentum_decay = 0.9
learn_rate = 0.2
weight_decay = 0.1
clip_limit = 100.0
norm_epsilon = 1e-07
coef_first = 3.4445
coef_second = -4.775
coef_third = 2.0315

def orthogonal_heads(moment, head_width):
    height = moment.shape[0]
    blocks = moment.reshape(height, -1, head_width)
    squares = lax.optimization_barrier(jnp.sum(blocks * blocks, axis=(0, 2)))
    blocks = blocks / (jnp.sqrt(squares) + norm_epsilon)[None, :, None]
    for iteration in range(ITERS):
        gram = jnp.einsum('rhi,rhj->hij', blocks, blocks, precision=lax.Precision.HIGHEST)
        mixer = coef_second * gram + coef_third * jnp.einsum('hij,hjk->hik', gram, gram, precision=lax.Precision.HIGHEST)
        blocks = coef_first * blocks + jnp.einsum('rhi,hij->rhj', blocks, mixer, precision=lax.Precision.HIGHEST)
    return blocks.reshape(height, -1)

def head_factors(gamma, head_width, rope_width):
    position = jnp.arange(head_width)
    root = jnp.sqrt(gamma)
    table = jnp.where(position[None, :] < head_width - rope_width, root[:, None], gamma[:, None])
    return table.reshape(-1)

def reference(grad_query, grad_key, query_weight, key_weight, query_moment, key_moment, max_logits):

    def accumulate(totals, pieces):
        return ((totals[0] + pieces[0].astype(jnp.float32), totals[1] + pieces[1].astype(jnp.float32)), None)
    start = (jnp.zeros(grad_query.shape[1:], jnp.float32), jnp.zeros(grad_key.shape[1:], jnp.float32))
    totals, unused = lax.scan(accumulate, start, (grad_query, grad_key))
    query_grad, key_grad = totals
    new_query_moment = momentum_decay * query_moment + query_grad
    new_key_moment = momentum_decay * key_moment + key_grad
    query_ortho = orthogonal_heads(new_query_moment, QH)
    key_ortho = orthogonal_heads(new_key_moment, KH)
    peak = lax.optimization_barrier(jnp.max(max_logits, axis=0))
    gamma = jnp.minimum(1.0, clip_limit / peak)
    query_scale = 0.2 * math.sqrt(max(QL, QH))
    key_scale = 0.2 * math.sqrt(max(KVL, KH))
    query_next = query_weight - learn_rate * (query_scale * query_ortho + weight_decay * query_weight)
    key_next = key_weight - learn_rate * (key_scale * key_ortho + weight_decay * key_weight)
    new_query_weight = (query_next * head_factors(gamma, QH, QROPE)[None, :]).astype(jnp.bfloat16)
    new_key_weight = (key_next * head_factors(gamma, KH, 0)[None, :]).astype(jnp.bfloat16)
    return (new_query_weight, new_key_weight, new_query_moment, new_key_moment)
```

```python
import functools
import math

import jax
import jax.numpy as jnp
from jax import lax
from jax.experimental import pallas as pl
from jax.experimental.pallas import tpu as pltpu
from jax.sharding import PartitionSpec as P

QL = 1536
KVL = 512
QH = 192
QROPE = 64
KH = 128
ITERS = 5

momentum_decay = 0.9
learn_rate = 0.2
weight_decay = 0.1
clip_limit = 100.0
norm_epsilon = 1e-07
coef_first = 3.4445
coef_second = -4.775
coef_third = 2.0315

N = 4
QC, KC = 384, 256
QR, KR = 192, 64
RA, RB, RC = 80, 80, 32
MC = RC * 3 + KR * 2
G_ROWS = 384
HQ, HK = QR // 2, KR // 2
H_ROWS = HQ * 3 + HK * 2

f32, bf16 = jnp.float32, jnp.bfloat16
AXES = ("dp", "ctx")
VMEM = pl.BlockSpec(memory_space=pltpu.VMEM)
SMEM = pl.BlockSpec(memory_space=pltpu.SMEM)
ANY = pl.BlockSpec(memory_space=pl.ANY)
HIGHEST = lax.Precision.HIGHEST


def place(z, x, y, c):
    return ((z % N) * N + x % N) * 2 * N + (y % N) * 2 + c


def send(array, target):
    pairs = [
        (place(z, x, y, c), place(*target(z, x, y, c)))
        for z in range(N)
        for x in range(N)
        for y in range(N)
        for c in range(2)
    ]
    return lax.ppermute(array, AXES, pairs)


def shift(array, axis, by):
    def target(z, x, y, c):
        return (z + by * (axis == "z"), x + by * (axis == "x"), y + by * (axis == "y"), c)

    return send(array, target)


def ring(array, axis):
    def target(z, x, y, c):
        by = 1 - 2 * c
        return (z + by * (axis == "z"), x + by * (axis == "x"), y + by * (axis == "y"), c)

    return send(array, target)


def swap(array):
    return send(array, lambda z, x, y, c: (z, x, y, 1 - c))


def exchange(array, axis, step):
    def target(z, x, y, c):
        return (
            z ^ (step * (axis == "z")),
            x ^ (step * (axis == "x")),
            y ^ (step * (axis == "y")),
            c,
        )

    return send(array, target)


def slice_copies(where, other, step, query, key, query_to, key_to, sems):
    z, x, y, core = where[0], where[1], where[2], where[3]
    if other:
        core = 1 - core
    ahead = (1 - 2 * core) * (N - step) + N
    block_a, block_b, block_c = (x + ahead) % N, (z + ahead) % N, (y + ahead) % N
    copies = ([], [], [])

    def add(part, source, to):
        number = sum(len(c) for c in copies)
        copies[part].append(pltpu.make_async_copy(source, to, sems.at[number]))

    def columns(zz, xx, width):
        return pl.ds(pl.multiple_of((zz * N + xx) * width, 128), width)

    for zz in range(N):
        add(
            0,
            query.at[:, core, pl.ds(0, RA), columns(zz, block_a, QC)],
            query_to.at[:, zz, pl.ds(0, RA), :],
        )
    for xx in range(N):
        add(
            1,
            query.at[:, core, pl.ds(RA, RB), columns(block_b, xx, QC)],
            query_to.at[xx, :, pl.ds(RA, RB), :],
        )
    for zz in range(N):
        for xx in range(N):
            add(
                2,
                query.at[block_c, core, pl.ds(RA + RB, RC), columns(zz, xx, QC)],
                query_to.at[zz, xx, pl.ds(RA + RB, RC), :],
            )
            add(2, key.at[block_c, core, :, columns(zz, xx, KC)], key_to.at[zz, xx])
    return copies


N_COPIES = 4 + 4 + 32


def slice_kernel(step, where, query, key, query_to, key_to, sems):
    copies = slice_copies(where, True, step, query, key, query_to, key_to, sems)
    for part in copies:
        for copy in part:
            copy.start()
    for part in copies:
        for copy in part:
            copy.wait()


def slice_other(step, where, query, key):
    return pl.pallas_call(
        functools.partial(slice_kernel, step),
        out_shape=(
            jax.ShapeDtypeStruct((N, N, QR, QC), bf16),
            jax.ShapeDtypeStruct((N, N, KR, KC), bf16),
        ),
        in_specs=[SMEM, ANY, ANY],
        out_specs=(ANY, ANY),
        scratch_shapes=[pltpu.SemaphoreType.DMA((N_COPIES,))],
        compiler_params=pltpu.CompilerParams(vmem_limit_bytes=4 << 20),
        name=f"slice_other_{step}",
    )(where, query, key)


def pre_kernel(step, where, query, key, query_from, key_from, a, b, c, own_q, own_k, sems):
    copies = slice_copies(where, False, step, query, key, own_q, own_k, sems)
    for part in copies:
        for copy in part:
            copy.start()

    def total(first, second):
        return (first.astype(f32) + second.astype(f32)).astype(bf16)

    def each(body):
        @pl.loop(0, N * N)
        def _(i):
            body(i // N, i % N)

    for copy in copies[0]:
        copy.wait()

    @each
    def _(i, j):
        rows = pl.ds(0, RA)
        a[i, j] = total(own_q[i, j, rows, :], query_from[i, j, rows, :])

    for copy in copies[1]:
        copy.wait()

    @each
    def _(i, j):
        rows = pl.ds(RA, RB)
        b[i, j] = total(own_q[i, j, rows, :], query_from[i, j, rows, :])

    for copy in copies[2]:
        copy.wait()

    @each
    def _(i, j):
        rows = pl.ds(RA + RB, RC)
        block = total(own_q[i, j, rows, :], query_from[i, j, rows, :])
        for lane in range(3):
            c[i, j, pl.ds(lane * RC, RC), :] = block[:, lane * 128 : (lane + 1) * 128]
        block = total(own_k[i, j], key_from[i, j])
        for lane in range(2):
            c[i, j, pl.ds(3 * RC + lane * KR, KR), :] = block[:, lane * 128 : (lane + 1) * 128]


def pre_sum(step, where, query, key, query_from, key_from):
    return pl.pallas_call(
        functools.partial(pre_kernel, step),
        out_shape=(
            jax.ShapeDtypeStruct((N, N, RA, QC), bf16),
            jax.ShapeDtypeStruct((N, N, RB, QC), bf16),
            jax.ShapeDtypeStruct((N, N, MC, 128), bf16),
        ),
        in_specs=[SMEM, ANY, ANY, VMEM, VMEM],
        out_specs=(VMEM, VMEM, VMEM),
        scratch_shapes=[
            pltpu.VMEM((N, N, QR, QC), bf16),
            pltpu.VMEM((N, N, KR, KC), bf16),
            pltpu.SemaphoreType.DMA((N_COPIES,)),
        ],
        compiler_params=pltpu.CompilerParams(vmem_limit_bytes=16 << 20),
        name=f"pre_sum_{step}",
    )(where, query, key, query_from, key_from)


def add(*terms):
    total = terms[0].astype(f32)
    for term in terms[1:]:
        total = total + term.astype(f32)
    return total.astype(bf16)


def block_of(array, index):
    return lax.dynamic_index_in_dim(array, index, 0, keepdims=False)


def scatter(array, axis, here):
    received = [shift(block_of(array, (here + by) % N), axis, by) for by in (1, 2, 3)]
    return [block_of(array, here)] + received


def moment_kernel(
    a0, a1, a2, a3, b0, b1, b2, b3, c0, c1, c2, c3, qm, km, qm_out, km_out, gram0, gram1
):
    def total(*refs):
        value = refs[0][...].astype(f32)
        for ref in refs[1:]:
            value = value + ref[...].astype(f32)
        return value

    part_c = total(c0, c1, c2, c3)
    qm_out[pl.ds(0, RA), :] = momentum_decay * qm[pl.ds(0, RA), :] + total(a0, a1, a2, a3)
    qm_out[pl.ds(RA, RB), :] = momentum_decay * qm[pl.ds(RA, RB), :] + total(b0, b1, b2, b3)
    for lane in range(3):
        lanes = pl.ds(lane * 128, 128)
        rows = pl.ds(RA + RB, RC)
        qm_out[rows, lanes] = (
            momentum_decay * qm[rows, lanes] + part_c[lane * RC : (lane + 1) * RC]
        )
    for lane in range(2):
        lanes = pl.ds(lane * 128, 128)
        start = 3 * RC + lane * KR
        km_out[:, lanes] = momentum_decay * km[:, lanes] + part_c[start : start + KR]

    def gram_of(value):
        return lax.dot_general(
            value, value, (((0,), (0,)), ((), ())), precision=HIGHEST, preferred_element_type=f32
        )

    full = qm_out[...]
    for head, out in enumerate((gram0, gram1)):
        wide = (full if head == 0 else pltpu.roll(full, QH, 1))[:, :256]
        gram = gram_of(wide)
        out[pl.ds(0, 192), :] = gram[:192, :128]
        out[pl.ds(192, 64), :] = gram[128:192, 128:]
        out[pl.ds(256, 128), :] = gram_of(km_out[:, pl.ds(head * KH, KH)])


def moments(parts_a, parts_b, parts_c, query_moment, key_moment):
    return pl.pallas_call(
        moment_kernel,
        out_shape=(
            jax.ShapeDtypeStruct((QR, QC), f32),
            jax.ShapeDtypeStruct((KR, KC), f32),
            jax.ShapeDtypeStruct((G_ROWS, 128), f32),
            jax.ShapeDtypeStruct((G_ROWS, 128), f32),
        ),
        in_specs=[VMEM] * 14,
        out_specs=(VMEM,) * 4,
        compiler_params=pltpu.CompilerParams(vmem_limit_bytes=16 << 20),
        name="moments",
    )(*parts_a, *parts_b, *parts_c, query_moment, key_moment)


def chain_kernel(g0, g1, g2, g3, out):
    packed = g0[...] + g1[...] + g2[...] + g3[...]
    top, side, corner = packed[:128], packed[128:192], packed[192:256]
    key_gram = packed[256:384]
    row = lax.broadcasted_iota(jnp.int32, (256, 256), 0)
    column = lax.broadcasted_iota(jnp.int32, (256, 256), 1)
    zeros = jnp.zeros((64, 128), f32)
    lower = jnp.concatenate([side, zeros], axis=0)
    query_gram = jnp.concatenate(
        [
            jnp.concatenate([top, lower.T], axis=1),
            jnp.concatenate([lower, jnp.concatenate([corner, zeros], axis=0)], axis=1),
        ],
        axis=0,
    )
    query_gram = jnp.where((row < QH) & (column < QH), query_gram, 0.0)
    query_eye = jnp.where((row == column) & (row < QH), 1.0, 0.0).astype(f32)
    key_eye = jnp.where(row == column, 1.0, 0.0).astype(f32)[:128, :128]

    def product(left, right):
        return jnp.dot(left, right, precision=HIGHEST, preferred_element_type=f32)

    def start(gram, eye):
        square = jnp.sum(jnp.sum(gram * eye, axis=1, keepdims=True), axis=0, keepdims=True)
        inverse = 1.0 / (jnp.sqrt(square) + norm_epsilon)
        return gram * inverse * inverse, inverse

    grams, inverses = zip(start(query_gram, query_eye), start(key_gram, key_eye))
    grams, eyes, totals = list(grams), (query_eye, key_eye), [None, None]
    for iteration in range(ITERS):
        mixers = []
        for i in range(2):
            square = product(grams[i], grams[i])
            mixers.append(coef_first * eyes[i] + coef_second * grams[i] + coef_third * square)
        if iteration < ITERS - 1:
            halves = [product(mixers[i], grams[i]) for i in range(2)]
        for i in range(2):
            totals[i] = mixers[i] if iteration == 0 else product(totals[i], mixers[i])
        if iteration < ITERS - 1:
            grams = [product(halves[i], mixers[i]) for i in range(2)]
    query_total, key_total = (totals[i] * inverses[i] for i in range(2))
    out[pl.ds(0, 192), :] = query_total[:192, :128]
    out[pl.ds(192, 192), :] = query_total[:192, 128:]
    out[pl.ds(384, 128), :] = key_total


def chain(grams):
    return pl.pallas_call(
        chain_kernel,
        out_shape=jax.ShapeDtypeStruct((512, 128), f32),
        in_specs=[VMEM] * 4,
        out_specs=VMEM,
        compiler_params=pltpu.CompilerParams(vmem_limit_bytes=16 << 20),
        name="newton_schulz_polynomial",
    )(*grams)


def update_kernel(where, own, other, qm, km, qw, kw, qf, kf, first, second):
    core = where[3]
    mine, theirs = own[...], other[...]
    packs = (jnp.where(core == 0, mine, theirs), jnp.where(core == 0, theirs, mine))

    def product(left, right):
        return jnp.dot(left, right, precision=HIGHEST, preferred_element_type=f32)

    full = qm[...]
    zeros = jnp.zeros((64, 256), f32)
    pad = jnp.zeros((QR, 128), f32)
    pieces = []
    for head in range(2):
        wide = (full if head == 0 else pltpu.roll(full, QH, 1))[:, :256]
        matrix = jnp.concatenate([packs[head][:192], packs[head][192:384]], axis=1)
        matrix = jnp.concatenate([matrix, zeros], axis=0)
        piece = jnp.concatenate([product(wide, matrix), pad], axis=1)
        pieces.append(piece if head == 0 else pltpu.roll(piece, QH, 1))
    query_ortho = pieces[0] + pieces[1]
    key_ortho = jnp.concatenate(
        [product(km[:, pl.ds(h * KH, KH)], packs[h][384:]) for h in range(2)], axis=1
    )
    query_scale = 0.2 * math.sqrt(max(QL, QH))
    key_scale = 0.2 * math.sqrt(max(KVL, KH))
    query_weight, key_weight = qw[...], kw[...]
    query_next = query_weight - learn_rate * (
        query_scale * query_ortho + weight_decay * query_weight
    )
    key_next = key_weight - learn_rate * (key_scale * key_ortho + weight_decay * key_weight)
    query_block = (query_next * qf[...]).astype(bf16)
    key_block = (key_next * kf[...]).astype(bf16)
    for half, out in enumerate((first, second)):
        for lane in range(3):
            out[pl.ds(lane * HQ, HQ), :] = query_block[
                half * HQ : (half + 1) * HQ, lane * 128 : (lane + 1) * 128
            ]
        for lane in range(2):
            out[pl.ds(3 * HQ + lane * HK, HK), :] = key_block[
                half * HK : (half + 1) * HK, lane * 128 : (lane + 1) * 128
            ]


def update(where, own, other, query_moment, key_moment, query_weight, key_weight, qf, kf):
    return pl.pallas_call(
        update_kernel,
        out_shape=(jax.ShapeDtypeStruct((H_ROWS, 128), bf16),) * 2,
        in_specs=[SMEM] + [VMEM] * 8,
        out_specs=(VMEM, VMEM),
        compiler_params=pltpu.CompilerParams(vmem_limit_bytes=16 << 20),
        name="update",
    )(where, own, other, query_moment, key_moment, query_weight, key_weight, qf, kf)


def assemble_kernel(where, *refs):
    z, x = where[0], where[1]
    inputs, (query_out, key_out) = refs[:8], refs[8:]
    for half in range(2):
        for far in range(N):
            stack = inputs[half * N + far]
            for near in range(N):
                if half == 0:
                    owner = ((z + N - near) % N) * N + (x + N - far) % N
                else:
                    owner = ((z + N - far) % N) * N + (x + N - near) % N
                for lane in range(3):
                    query_out[
                        pl.ds(half * HQ, HQ),
                        pl.ds(pl.multiple_of(owner * QC + lane * 128, 128), 128),
                    ] = stack[near, pl.ds(lane * HQ, HQ), :]
                for lane in range(2):
                    key_out[
                        pl.ds(half * HK, HK),
                        pl.ds(pl.multiple_of(owner * KC + lane * 128, 128), 128),
                    ] = stack[near, pl.ds(3 * HQ + lane * HK, HK), :]


def assemble(where, first, second):
    return pl.pallas_call(
        assemble_kernel,
        out_shape=(
            jax.ShapeDtypeStruct((QR, N * N * QC), bf16),
            jax.ShapeDtypeStruct((KR, N * N * KC), bf16),
        ),
        in_specs=[SMEM] + [VMEM] * 8,
        out_specs=(VMEM, VMEM),
        compiler_params=pltpu.CompilerParams(vmem_limit_bytes=20 << 20),
        name="assemble",
    )(where, *first, *second)


def gather(array, axis):
    return [array] + [shift(array, axis, by) for by in (1, 2, 3)]


def head_factors(gamma, head_width, rope_width):
    position = jnp.arange(head_width)
    root = jnp.sqrt(gamma)
    table = jnp.where(position[None, :] < head_width - rope_width, root[:, None], gamma[:, None])
    return table.reshape(1, -1)


def on_device(grad_query, grad_key, query_weight, key_weight, query_moment, key_moment, max_logits):
    dp, ctx = lax.axis_index("dp"), lax.axis_index("ctx")
    z, x, y, core = dp // N, dp % N, ctx // 2, ctx % 2
    where = jnp.stack([z, x, y, core]).astype(jnp.int32)
    query = grad_query.reshape(N, 2, QR, N * N * QC)
    key = grad_key.reshape(N, 2, KR, N * N * KC)

    pre = []
    for step in range(1, N + 1):
        query_part, key_part = slice_other(step, where, query, key)
        query_part, key_part = swap(query_part), swap(key_part)
        pre.append(pre_sum(step, where, query, key, query_part, key_part))

    sums = list(pre[0])
    for step in range(1, N):
        sums = [ring(part, axis) for part, axis in zip(sums, ("x", "z", "y"))]
        sums = [add(own, part) for own, part in zip(pre[step], sums)]

    peak = max_logits[0]
    peak = jnp.maximum(peak, swap(peak))
    for axis in ("x", "y", "z"):
        for step in (1, 2):
            peak = jnp.maximum(peak, exchange(peak, axis, step))
    gamma = jnp.minimum(1.0, clip_limit / peak)
    gamma = lax.dynamic_slice_in_dim(gamma, dp * 2, 2, 0)
    query_factor, key_factor = head_factors(gamma, QH, QROPE), head_factors(gamma, KH, 0)

    here = dict(z=z, x=x, y=y)
    second = [scatter(s, axis, here[axis]) for s, axis in zip(sums, ("y", "x", "z"))]
    sums = [add(*terms) for terms in second]
    third = [scatter(s, axis, here[axis]) for s, axis in zip(sums, ("z", "y", "x"))]
    new_query_moment, new_key_moment, gram0, gram1 = moments(*third, query_moment, key_moment)

    keep, give = jnp.where(core == 0, gram0, gram1), jnp.where(core == 0, gram1, gram0)
    gram = keep + swap(give)
    own = chain(gather(gram, "y"))
    first, last = update(
        where,
        own,
        swap(own),
        new_query_moment,
        new_key_moment,
        query_weight,
        key_weight,
        query_factor,
        key_factor,
    )
    first, last = jnp.stack(gather(first, "z")), jnp.stack(gather(last, "x"))
    first, last = gather(first, "x"), gather(last, "z")
    query_out, key_out = assemble(where, first, last)
    return (query_out, key_out, new_query_moment, new_key_moment)


def solution(mesh):
    in_specs = (
        P(("dp", "ctx"), None, None),
        P(("dp", "ctx"), None, None),
        P("ctx", "dp"),
        P("ctx", "dp"),
        P("ctx", "dp"),
        P("ctx", "dp"),
        P(("dp", "ctx"), None),
    )
    out_specs = (P("ctx", None), P("ctx", None), P("ctx", "dp"), P("ctx", "dp"))
    return jax.shard_map(
        on_device, mesh=mesh, in_specs=in_specs, out_specs=out_specs, check_vma=False
    )
```

```python
import functools
import math

import jax
import jax.numpy as jnp
from jax import lax
from jax.experimental import pallas as pl
from jax.experimental.pallas import tpu as pltpu
from jax.sharding import PartitionSpec as P

QL = 1536
KVL = 512
QH = 192
QROPE = 64
KH = 128
ITERS = 5

momentum_decay = 0.9
learn_rate = 0.2
weight_decay = 0.1
clip_limit = 100.0
norm_epsilon = 1e-07
coef_first = 3.4445
coef_second = -4.775
coef_third = 2.0315

N = 4
QC, KC = 384, 256
QR, KR = 192, 64
RP, RC = 80, 32
MP = RP * 3
MC = RC * 3 + KR * 2
ML = 16
M_ALL = 2 * MP + MC
G_ROWS = 384

f32, bf16 = jnp.float32, jnp.bfloat16
AXES = ("dp", "ctx")
VMEM = pl.BlockSpec(memory_space=pltpu.VMEM)
SMEM = pl.BlockSpec(memory_space=pltpu.SMEM)
HBM = pl.BlockSpec(memory_space=pltpu.HBM)
HIGHEST = lax.Precision.HIGHEST


def params(mib):
    return pltpu.CompilerParams(vmem_limit_bytes=mib << 20)


def out(shape, dtype):
    return jax.ShapeDtypeStruct(shape, dtype)


def place(z, x, y, c):
    return ((z % N) * N + x % N) * 2 * N + (y % N) * 2 + c


def shift(array, axes, steps):
    def target(z, x, y, c):
        axis, by = axes[c], steps[c]
        return (z + by * (axis == "z"), x + by * (axis == "x"), y + by * (axis == "y"), c)

    pairs = [
        (place(z, x, y, c), place(*target(z, x, y, c)))
        for z in range(N)
        for x in range(N)
        for y in range(N)
        for c in range(2)
    ]
    return lax.ppermute(array, AXES, pairs)


def swap(array):
    pairs = [(i, i ^ 1) for i in range(2 * N**3)]
    return lax.ppermute(array, AXES, pairs)


def read(where):
    return where[0], where[1], where[2], where[3]


def columns(zz, xx, width, lane=None):
    start = (zz * N + xx) * width
    if lane is None:
        return pl.ds(pl.multiple_of(start, 128), width)
    return pl.ds(pl.multiple_of(start + lane * 128, 128), 128)


def slice_copies(where, other, step, query, key, logits, scratch):
    blocks, c_query, c_key, own_logits, sems = scratch
    z, x, y, core = read(where)
    if other:
        core = 1 - core
    ahead = N - step
    here = jnp.where(core == 0, x, z) + N
    block_c = (y + (1 - 2 * core) * ahead + N) % N
    main = []
    for i in range(N):
        for owner, block in ((0, (here + ahead) % N), (1, (here - ahead) % N)):
            start = jnp.where(core == 0, i * N + block, block * N + i) * QC
            main.append(
                pltpu.make_async_copy(
                    query.at[
                        :,
                        owner,
                        pl.ds(pl.multiple_of(core * RP, 16), RP),
                        pl.ds(pl.multiple_of(start, 128), QC),
                    ],
                    blocks.at[owner, i],
                    sems.at[owner * N + i],
                )
            )
    rest = [pltpu.make_async_copy(logits, own_logits, sems.at[2 * N])]
    for half in range(2):
        rows = pl.ds(half * RC // 2, RC // 2)
        rest.append(
            pltpu.make_async_copy(
                query.at[block_c, core, pl.ds(2 * RP + half * RC // 2, RC // 2), :],
                c_query.at[rows, :],
                sems.at[2 * N + 1 + 2 * half],
            )
        )
        rows = pl.ds(half * KR // 2, KR // 2)
        rest.append(
            pltpu.make_async_copy(
                key.at[block_c, core, rows, :],
                c_key.at[rows, :],
                sems.at[2 * N + 2 + 2 * half],
            )
        )
    return core, main, rest


def split_logits(value):
    high = value.astype(bf16)
    rest = value - high.astype(f32)
    middle = rest.astype(bf16)
    low = (rest - middle.astype(f32)).astype(bf16)
    return high, middle, low


def join_logits(rows):
    rows = rows.astype(f32)
    return rows[0:1] + rows[1:2] + rows[2:3]


def logit_rows(value):
    high, middle, low = (part.astype(f32) for part in split_logits(value))
    row = lax.broadcasted_iota(jnp.int32, (ML, 128), 0)
    return jnp.where(row == 0, high, jnp.where(row == 1, middle, jnp.where(row == 2, low, 0.0)))


def slice_kernel(step, where, query, key, logits, to, *scratch):
    scratch, lanes = scratch[:-1], scratch[-1]
    blocks, c_query, c_key, own_logits, _ = scratch
    core, main, rest = slice_copies(where, True, step, query, key, logits, scratch)
    for copy in rest + main:
        copy.start()
    lanes[...] = jnp.zeros_like(lanes)
    for copy in rest:
        copy.wait()
    lanes[pl.ds(0, 1), pl.ds(0, 32)] = own_logits[...]
    logit_block = logit_rows(lanes[pl.ds(0, 1), :]).astype(bf16)

    @pl.loop(0, N * N)
    def _(i):
        at = (i // N, i % N)
        to[at + (pl.ds(M_ALL, ML),)] = logit_block
        for source, height, width, start, size in (
            (c_query, RC, 3, 0, QC),
            (c_key, KR, 2, 3 * RC, KC),
        ):
            for lane in range(width):
                to[at + (pl.ds(2 * MP + start + lane * height, height),)] = source[
                    :, columns(at[0], at[1], size, lane)
                ]

    for i in range(N):
        main[2 * i].wait()
        main[2 * i + 1].wait()

        @pl.loop(0, N)
        def _(j):
            first, second = jnp.where(core == 0, j, i), jnp.where(core == 0, i, j)
            for owner in range(2):
                block = blocks[owner, i, j]
                for lane in range(3):
                    to[first, second, pl.ds(owner * MP + lane * RP, RP), :] = block[
                        :, lane * 128 : (lane + 1) * 128
                    ]


def slice_scratch():
    return [
        pltpu.VMEM((2, N, N, RP, QC), bf16),
        pltpu.VMEM((RC, N * N * QC), bf16),
        pltpu.VMEM((KR, N * N * KC), bf16),
        pltpu.VMEM((1, 32), f32),
        pltpu.SemaphoreType.DMA((2 * N + 5,)),
        pltpu.VMEM((8, 128), f32),
    ]


def in_hbm(*arrays):
    return tuple(pltpu.with_memory_space_constraint(a, pltpu.HBM) for a in arrays)


def in_hbm(*arrays):
    return tuple(pltpu.with_memory_space_constraint(a, pltpu.HBM) for a in arrays)


def slice_other(step, where, query, key, logits):
    return pl.pallas_call(
        functools.partial(slice_kernel, step),
        out_shape=out((N, N, M_ALL + ML, 128), bf16),
        in_specs=[SMEM, HBM, HBM, HBM],
        out_specs=VMEM,
        scratch_shapes=slice_scratch(),
        compiler_params=params(8),
        name=f"slice_other_{step}",
    )(where, *in_hbm(query, key, logits))


def total(*terms):
    value = terms[0].astype(f32)
    for term in terms[1:]:
        value = value + term.astype(f32)
    return value


def most(*terms):
    value = join_logits(terms[0])
    for term in terms[1:]:
        value = jnp.maximum(value, join_logits(term))
    return logit_rows(value)


def pre_kernel(step, where, query, key, logits, other, p, m, c, *scratch):
    scratch, lanes = scratch[:-1], scratch[-1]
    blocks, c_query, c_key, own_logits, _ = scratch
    core, main, rest = slice_copies(where, False, step, query, key, logits, scratch)
    for copy in rest + main:
        copy.start()
    lanes[...] = jnp.zeros_like(lanes)
    for copy in rest:
        copy.wait()
    lanes[pl.ds(0, 1), pl.ds(0, 32)] = own_logits[...]
    peak = jnp.maximum(
        lanes[pl.ds(0, 1), :], join_logits(other[0, 0, pl.ds(M_ALL, ML), :])
    )
    logit_block = logit_rows(peak).astype(bf16)

    @pl.loop(0, N * N)
    def _(i):
        at = (i // N, i % N)
        c[at + (pl.ds(MC, ML),)] = logit_block
        for source, height, width, start, size in (
            (c_query, RC, 3, 0, QC),
            (c_key, KR, 2, 3 * RC, KC),
        ):
            for lane in range(width):
                rows = start + lane * height
                c[at + (pl.ds(rows, height),)] = total(
                    source[:, columns(at[0], at[1], size, lane)],
                    other[at + (pl.ds(2 * MP + rows, height),)],
                ).astype(bf16)

    for i in range(N):
        main[2 * i].wait()
        main[2 * i + 1].wait()

        @pl.loop(0, N)
        def _(j):
            first, second = jnp.where(core == 0, j, i), jnp.where(core == 0, i, j)
            for owner, to in ((0, p), (1, m)):
                block = blocks[owner, i, j]
                for lane in range(3):
                    to[first, second, pl.ds(lane * RP, RP), :] = total(
                        block[:, lane * 128 : (lane + 1) * 128],
                        other[first, second, pl.ds(owner * MP + lane * RP, RP), :],
                    ).astype(bf16)


def pre_sum(step, where, query, key, logits, other):
    return pl.pallas_call(
        functools.partial(pre_kernel, step),
        out_shape=[out((N, N, height, 128), bf16) for height in (MP, MP, MC + ML)],
        in_specs=[SMEM, HBM, HBM, HBM, VMEM],
        out_specs=[VMEM] * 3,
        scratch_shapes=slice_scratch(),
        compiler_params=params(12),
        name=f"pre_sum_{step}",
    )(where, *in_hbm(query, key, logits), other)


def ring_add_kernel(p0, m0, c0, p1, m1, c1, p, m, c):
    peak = most(c0[0, 0, pl.ds(MC, ML), :], c1[0, 0, pl.ds(MC, ML), :]).astype(bf16)

    @pl.loop(0, N * N)
    def _(i):
        at = (i // N, i % N)
        p[at] = total(p0[at], p1[at]).astype(bf16)
        m[at] = total(m0[at], m1[at]).astype(bf16)
        rows = at + (pl.ds(0, MC),)
        c[rows] = total(c0[rows], c1[rows]).astype(bf16)
        c[at + (pl.ds(MC, ML),)] = peak


def ring_add(own, received):
    return pl.pallas_call(
        ring_add_kernel,
        out_shape=[out(a.shape, bf16) for a in own],
        in_specs=[VMEM] * 6,
        out_specs=[VMEM] * 3,
        compiler_params=params(14),
        name="ring_add",
    )(*own, *received)


def split_ab_kernel(where, p0, m0, p1, m1, *outs):
    _, x, y, core = read(where)
    here = jnp.where(core == 0, y, x)
    for by, to in enumerate(outs):
        block = (here + by) % N

        @pl.loop(0, N)
        def _(i):
            to[i, pl.ds(0, MP), :] = total(p0[block, i], p1[block, i]).astype(bf16)
            to[i, pl.ds(MP, MP), :] = total(m0[block, i], m1[block, i]).astype(bf16)


def split_ab(where, own, received):
    return pl.pallas_call(
        split_ab_kernel,
        out_shape=[out((N, 2 * MP, 128), bf16)] * N,
        in_specs=[SMEM] + [VMEM] * 4,
        out_specs=[VMEM] * N,
        compiler_params=params(10),
        name="split_ab",
    )(where, *own, *received)


def split_c_kernel(where, c0, c1, *outs):
    peak = most(c0[0, 0, pl.ds(MC, ML), :], c1[0, 0, pl.ds(MC, ML), :]).astype(bf16)
    for by, to in enumerate(outs):
        block = (where[0] + by) % N

        @pl.loop(0, N)
        def _(i):
            rows = (block, i, pl.ds(0, MC))
            to[i, pl.ds(0, MC), :] = total(c0[rows], c1[rows]).astype(bf16)
            to[i, pl.ds(MC, ML), :] = peak


def split_c(where, own, received):
    return pl.pallas_call(
        split_c_kernel,
        out_shape=[out((N, MC + ML, 128), bf16)] * N,
        in_specs=[SMEM] + [VMEM] * 2,
        out_specs=[VMEM] * N,
        compiler_params=params(6),
        name="split_c",
    )(where, own, received)


def next_ab_kernel(where, t0, t1, t2, t3, *outs):
    z, _, y, core = read(where)
    here = jnp.where(core == 0, z, y)
    for by, to in enumerate(outs):
        block = (here + by) % N
        to[...] = total(t0[block], t1[block], t2[block], t3[block]).astype(bf16)


def next_c_kernel(where, t0, t1, t2, t3, *outs):
    terms = (t0, t1, t2, t3)
    peak = most(*(t[0, pl.ds(MC, ML), :] for t in terms)).astype(bf16)
    for by, to in enumerate(outs):
        rows = ((where[1] + by) % N, pl.ds(0, MC))
        to[pl.ds(0, MC), :] = total(*(t[rows] for t in terms)).astype(bf16)
        to[pl.ds(MC, ML), :] = peak


def next_parts(kernel, name, where, terms):
    return pl.pallas_call(
        kernel,
        out_shape=[out((terms[0].shape[1], 128), bf16)] * N,
        in_specs=[SMEM] + [VMEM] * N,
        out_specs=[VMEM] * N,
        compiler_params=params(6),
        name=name,
    )(where, *terms)


def scatter(blocks, axes):
    return [blocks[0]] + [shift(blocks[by], axes, (by, by)) for by in (1, 2, 3)]


def moment_kernel(
    where, a0, a1, a2, a3, c0, c1, c2, c3, qm, theirs, km, qm_out, km_out, gram0, gram1, peak
):
    core = where[3]
    part = total(a0[...], a1[...], a2[...], a3[...])
    rows = pl.ds(0, MC)
    part_c = total(c0[rows, :], c1[rows, :], c2[rows, :], c3[rows, :])
    rows = pl.ds(MC, ML)
    value = join_logits(c0[rows, :])
    for ref in (c1, c2, c3):
        value = jnp.maximum(value, join_logits(ref[rows, :]))
    peak[...] = jnp.broadcast_to(value, (8, 128))
    for lane in range(3):
        lanes = pl.ds(lane * 128, 128)
        for owner in range(2):
            rows = pl.ds(owner * RP, RP)
            start = owner * MP + lane * RP
            moment = jnp.where(core == owner, qm[rows, lanes], theirs[:, lanes])
            qm_out[rows, lanes] = momentum_decay * moment + part[start : start + RP]
        rows = pl.ds(2 * RP, RC)
        qm_out[rows, lanes] = (
            momentum_decay * qm[rows, lanes] + part_c[lane * RC : (lane + 1) * RC]
        )
    for lane in range(2):
        lanes = pl.ds(lane * 128, 128)
        start = 3 * RC + lane * KR
        km_out[:, lanes] = momentum_decay * km[:, lanes] + part_c[start : start + KR]

    def gram_of(value):
        return lax.dot_general(
            value, value, (((0,), (0,)), ((), ())), precision=HIGHEST, preferred_element_type=f32
        )

    full = qm_out[...]
    for head, to in enumerate((gram0, gram1)):
        wide = (full if head == 0 else pltpu.roll(full, QH, 1))[:, :256]
        gram = gram_of(wide)
        to[pl.ds(0, 192), :] = gram[:192, :128]
        to[pl.ds(192, 64), :] = gram[128:192, 128:]
        to[pl.ds(256, 128), :] = gram_of(km_out[:, pl.ds(head * KH, KH)])


def moments(where, part, part_c, query_moment, theirs, key_moment):
    return pl.pallas_call(
        moment_kernel,
        out_shape=(
            out((QR, QC), f32),
            out((KR, KC), f32),
            out((G_ROWS, 128), f32),
            out((G_ROWS, 128), f32),
            out((8, 128), f32),
        ),
        in_specs=[SMEM] + [VMEM] * 11,
        out_specs=(VMEM,) * 5,
        compiler_params=params(12),
        name="moments",
    )(where, *part, *part_c, query_moment, theirs, key_moment)


def chain_kernel(g0, g1, g2, g3, to):
    packed = g0[...] + g1[...] + g2[...] + g3[...]
    top, side, corner = packed[:128], packed[128:192], packed[192:256]
    key_gram = packed[256:384]
    row = lax.broadcasted_iota(jnp.int32, (256, 256), 0)
    column = lax.broadcasted_iota(jnp.int32, (256, 256), 1)
    zeros = jnp.zeros((64, 128), f32)
    lower = jnp.concatenate([side, zeros], axis=0)
    query_gram = jnp.concatenate(
        [
            jnp.concatenate([top, lower.T], axis=1),
            jnp.concatenate([lower, jnp.concatenate([corner, zeros], axis=0)], axis=1),
        ],
        axis=0,
    )
    query_gram = jnp.where((row < QH) & (column < QH), query_gram, 0.0)
    query_eye = jnp.where((row == column) & (row < QH), 1.0, 0.0).astype(f32)
    key_eye = jnp.where(row == column, 1.0, 0.0).astype(f32)[:128, :128]

    def product(left, right):
        return jnp.dot(left, right, precision=HIGHEST, preferred_element_type=f32)

    def start(gram, eye):
        square = jnp.sum(jnp.sum(gram * eye, axis=1, keepdims=True), axis=0, keepdims=True)
        inverse = 1.0 / (jnp.sqrt(square) + norm_epsilon)
        return gram * inverse * inverse, inverse

    grams, inverses = zip(start(query_gram, query_eye), start(key_gram, key_eye))
    grams, eyes, totals = list(grams), (query_eye, key_eye), [None, None]
    for iteration in range(ITERS):
        mixers = []
        for i in range(2):
            square = product(grams[i], grams[i])
            mixers.append(coef_first * eyes[i] + coef_second * grams[i] + coef_third * square)
        if iteration < ITERS - 1:
            halves = [product(mixers[i], grams[i]) for i in range(2)]
        for i in range(2):
            totals[i] = mixers[i] if iteration == 0 else product(totals[i], mixers[i])
        if iteration < ITERS - 1:
            grams = [product(halves[i], mixers[i]) for i in range(2)]
    query_total, key_total = (totals[i] * inverses[i] for i in range(2))
    to[pl.ds(0, 192), :] = query_total[:192, :128]
    to[pl.ds(192, 192), :] = query_total[:192, 128:]
    to[pl.ds(384, 128), :] = key_total


def chain(grams):
    return pl.pallas_call(
        chain_kernel,
        out_shape=out((512, 128), f32),
        in_specs=[VMEM] * 4,
        out_specs=VMEM,
        compiler_params=params(12),
        name="newton_schulz_polynomial",
    )(*grams)

def update_kernel(where, own, other, peak, qm, km, qw, kw, to):
    z, x, _, core = read(where)
    mine, theirs = own[...], other[...]
    packs = (jnp.where(core == 0, mine, theirs), jnp.where(core == 0, theirs, mine))

    def product(left, right):
        return jnp.dot(left, right, precision=HIGHEST, preferred_element_type=f32)

    gamma = jnp.minimum(1.0, clip_limit / peak[pl.ds(0, 1), :])
    lane = lax.broadcasted_iota(jnp.int32, (1, 128), 1)
    first_head = 2 * (z * N + x)
    gammas = [
        jnp.sum(jnp.where(lane == first_head + h, gamma, 0.0), axis=1, keepdims=True)
        for h in range(2)
    ]
    roots = [jnp.sqrt(g) for g in gammas]
    column = lax.broadcasted_iota(jnp.int32, (1, QC), 1)
    second = column >= QH
    rope = jnp.where(second, column - QH, column) >= QH - QROPE
    query_factor = jnp.where(
        rope, jnp.where(second, gammas[1], gammas[0]), jnp.where(second, roots[1], roots[0])
    )
    key_factor = jnp.where(
        lax.broadcasted_iota(jnp.int32, (1, KC), 1) >= KH, roots[1], roots[0]
    )

    full = qm[...]
    zeros = jnp.zeros((64, 256), f32)
    pad = jnp.zeros((QR, 128), f32)
    pieces = []
    for head in range(2):
        wide = (full if head == 0 else pltpu.roll(full, QH, 1))[:, :256]
        matrix = jnp.concatenate([packs[head][:192], packs[head][192:384]], axis=1)
        matrix = jnp.concatenate([matrix, zeros], axis=0)
        piece = jnp.concatenate([product(wide, matrix), pad], axis=1)
        pieces.append(piece if head == 0 else pltpu.roll(piece, QH, 1))
    query_ortho = pieces[0] + pieces[1]
    key_ortho = jnp.concatenate(
        [product(km[:, pl.ds(h * KH, KH)], packs[h][384:]) for h in range(2)], axis=1
    )
    query_scale = 0.2 * math.sqrt(max(QL, QH))
    key_scale = 0.2 * math.sqrt(max(KVL, KH))
    query_weight, key_weight = qw[...], kw[...]
    query_next = query_weight - learn_rate * (
        query_scale * query_ortho + weight_decay * query_weight
    )
    key_next = key_weight - learn_rate * (key_scale * key_ortho + weight_decay * key_weight)
    query_block = (query_next * query_factor).astype(bf16)
    key_block = (key_next * key_factor).astype(bf16)
    for lane in range(3):
        to[pl.ds(lane * QR, QR), :] = query_block[:, lane * 128 : (lane + 1) * 128]
    for lane in range(2):
        to[pl.ds(3 * QR + lane * KR, KR), :] = key_block[:, lane * 128 : (lane + 1) * 128]


def update(where, own, other, peak, query_moment, key_moment, query_weight, key_weight):
    return pl.pallas_call(
        update_kernel,
        out_shape=out((M_ALL, 128), bf16),
        in_specs=[SMEM] + [VMEM] * 7,
        out_specs=VMEM,
        compiler_params=params(12),
        name="update",
    )(where, own, other, peak, query_moment, key_moment, query_weight, key_weight)


def assemble_kernel(where, s0, s1, s2, s3, query_out, key_out):
    z, x, _, core = read(where)
    for far, stack in enumerate((s0, s1, s2, s3)):

        @pl.loop(0, N)
        def _(near):
            back_z = jnp.where(core == 0, near, far)
            back_x = jnp.where(core == 0, far, near)
            zz, xx = (z + N - back_z) % N, (x + N - back_x) % N
            for lane in range(3):
                query_out[:, columns(zz, xx, QC, lane)] = stack[near, pl.ds(lane * QR, QR), :]
            for lane in range(2):
                key_out[:, columns(zz, xx, KC, lane)] = stack[
                    near, pl.ds(3 * QR + lane * KR, KR), :
                ]


def assemble(where, stacks):
    return pl.pallas_call(
        assemble_kernel,
        out_shape=(out((QR, N * N * QC), bf16), out((KR, N * N * KC), bf16)),
        in_specs=[SMEM] + [VMEM] * N,
        out_specs=(VMEM, VMEM),
        compiler_params=params(16),
        name="assemble",
    )(where, *stacks)


def on_device(grad_query, grad_key, query_weight, key_weight, query_moment, key_moment, max_logits):
    dp, ctx = lax.axis_index("dp"), lax.axis_index("ctx")
    z, x, y, core = dp // N, dp % N, ctx // 2, ctx % 2
    where = jnp.stack([z, x, y, core]).astype(jnp.int32)
    query = grad_query.reshape(N, 2, QR, N * N * QC)
    key = grad_key.reshape(N, 2, KR, N * N * KC)

    def after(value):
        return lax.optimization_barrier((where, value))[0]

    first = slice_other(1, where, query, key, max_logits)
    second = slice_other(2, after(first), query, key, max_logits)
    others, pre = [swap(first), swap(second)], []
    for step in range(1, N + 1):
        pre.append(pre_sum(step, where, query, key, max_logits, others[step - 1]))
        if step + 2 <= N:
            blocks = slice_other(step + 2, after(pre[-1][2]), query, key, max_logits)
            others.append(swap(blocks))

    parts = pre[0]
    for step in range(1, N):
        p, m, c = parts
        p = shift(p, ("x", "z"), (1, 1))
        m = shift(m, ("x", "z"), (-1, -1))
        c = shift(c, ("y", "y"), (1, -1))
        if step < N - 1:
            parts = ring_add(pre[step], (p, m, c))
        if step == 1:
            start = (1 - after(parts[0])[3]) * RP
            theirs = swap(lax.dynamic_slice_in_dim(query_moment, start, RP, 0))
        if step == 2:
            theirs, parts = lax.optimization_barrier((theirs, parts))
    pre = pre[-1]

    part = split_ab(where, pre[:2], (p, m))
    part_c = split_c(after(part[0]), pre[2], c)
    part, part_c = scatter(part, ("y", "x")), scatter(part_c, ("z", "z"))
    part = next_parts(next_ab_kernel, "next_ab", where, part)
    part_c = next_parts(next_c_kernel, "next_c", after(part[0]), part_c)
    part, part_c = scatter(part, ("z", "y")), scatter(part_c, ("x", "x"))
    moment, new_key_moment, gram0, gram1, peak = moments(
        where, part, part_c, query_moment, theirs, key_moment
    )

    keep, give = jnp.where(core == 0, gram0, gram1), jnp.where(core == 0, gram1, gram0)
    gram = keep + swap(give)
    own = chain([gram] + [shift(gram, ("y", "y"), (by, by)) for by in (1, 2, 3)])

    theirs = swap(lax.dynamic_slice_in_dim(moment, (1 - core) * RP, RP, 0))
    new_query_moment = jnp.concatenate(
        [
            jnp.where(core == 0, moment[:RP], theirs),
            jnp.where(core == 0, theirs, moment[RP : 2 * RP]),
            moment[2 * RP :],
        ]
    )
    block = update(
        where, own, swap(own), peak, new_query_moment, new_key_moment, query_weight, key_weight
    )
    stack = jnp.stack([block] + [shift(block, ("z", "x"), (by, by)) for by in (1, 2, 3)])
    stacks = [stack] + [shift(stack, ("x", "z"), (by, by)) for by in (1, 2, 3)]
    query_out, key_out = assemble(where, stacks)
    return (query_out, key_out, new_query_moment, new_key_moment)


def solution(mesh):
    in_specs = (
        P(("dp", "ctx"), None, None),
        P(("dp", "ctx"), None, None),
        P("ctx", "dp"),
        P("ctx", "dp"),
        P("ctx", "dp"),
        P("ctx", "dp"),
        P(("dp", "ctx"), None),
    )
    out_specs = (P("ctx", None), P("ctx", None), P("ctx", "dp"), P("ctx", "dp"))
    return jax.shard_map(
        on_device, mesh=mesh, in_specs=in_specs, out_specs=out_specs, check_vma=False
    )
```

```python
import functools
import math

import jax
import jax.numpy as jnp
from jax import lax
from jax.experimental import pallas as pl
from jax.experimental.pallas import tpu as pltpu
from jax.sharding import PartitionSpec as P

QL = 1536
KVL = 512
QH = 192
QROPE = 64
KH = 128
ITERS = 5

momentum_decay = 0.9
learn_rate = 0.2
weight_decay = 0.1
clip_limit = 100.0
norm_epsilon = 1e-07
coef_first = 3.4445
coef_second = -4.775
coef_third = 2.0315

N = 4
QC, KC = 384, 256
QR, KR = 192, 64
RP, RC = 80, 32
MP = RP * 3
MC = RC * 3 + KR * 2
ML = 16
M_ALL = 2 * MP + MC
M_HALF = M_ALL // 2
G_ROWS = 384

f32, bf16 = jnp.float32, jnp.bfloat16
AXES = ("dp", "ctx")
VMEM = pl.BlockSpec(memory_space=pltpu.VMEM)
SMEM = pl.BlockSpec(memory_space=pltpu.SMEM)
HBM = pl.BlockSpec(memory_space=pltpu.HBM)
HIGHEST = lax.Precision.HIGHEST


def params(mib):
    return pltpu.CompilerParams(vmem_limit_bytes=mib << 20)


def out(shape, dtype):
    return jax.ShapeDtypeStruct(shape, dtype)


def place(z, x, y, c):
    return ((z % N) * N + x % N) * 2 * N + (y % N) * 2 + c


def shift(array, axes, steps):
    def target(z, x, y, c):
        axis, by = axes[c], steps[c]
        return (z + by * (axis == "z"), x + by * (axis == "x"), y + by * (axis == "y"), c)

    pairs = [
        (place(z, x, y, c), place(*target(z, x, y, c)))
        for z in range(N)
        for x in range(N)
        for y in range(N)
        for c in range(2)
    ]
    return lax.ppermute(array, AXES, pairs)


def swap(array):
    pairs = [(i, i ^ 1) for i in range(2 * N**3)]
    return lax.ppermute(array, AXES, pairs)


def read(where):
    return where[0], where[1], where[2], where[3]


def columns(zz, xx, width, lane=None):
    start = (zz * N + xx) * width
    if lane is None:
        return pl.ds(pl.multiple_of(start, 128), width)
    return pl.ds(pl.multiple_of(start + lane * 128, 128), 128)


def slice_copies(where, other, step, query, key, logits, scratch):
    blocks, c_query, c_key, own_logits, sems = scratch
    z, x, y, core = read(where)
    if other:
        core = 1 - core
    ahead = N - step
    here = jnp.where(core == 0, x, z) + N
    block_c = (y + (1 - 2 * core) * ahead + N) % N
    main = []
    for i in range(N):
        for owner, block in ((0, (here + ahead) % N), (1, (here - ahead) % N)):
            start = jnp.where(core == 0, i * N + block, block * N + i) * QC
            main.append(
                pltpu.make_async_copy(
                    query.at[
                        :,
                        owner,
                        pl.ds(pl.multiple_of(core * RP, 16), RP),
                        pl.ds(pl.multiple_of(start, 128), QC),
                    ],
                    blocks.at[owner, i],
                    sems.at[owner * N + i],
                )
            )
    rest = [pltpu.make_async_copy(logits, own_logits, sems.at[2 * N])]
    for half in range(2):
        rows = pl.ds(half * RC // 2, RC // 2)
        rest.append(
            pltpu.make_async_copy(
                query.at[block_c, core, pl.ds(2 * RP + half * RC // 2, RC // 2), :],
                c_query.at[rows, :],
                sems.at[2 * N + 1 + 2 * half],
            )
        )
        rows = pl.ds(half * KR // 2, KR // 2)
        rest.append(
            pltpu.make_async_copy(
                key.at[block_c, core, rows, :],
                c_key.at[rows, :],
                sems.at[2 * N + 2 + 2 * half],
            )
        )
    return core, main, rest


def split_logits(value):
    high = value.astype(bf16)
    rest = value - high.astype(f32)
    middle = rest.astype(bf16)
    low = (rest - middle.astype(f32)).astype(bf16)
    return high, middle, low


def join_logits(rows):
    rows = rows.astype(f32)
    return rows[0:1] + rows[1:2] + rows[2:3]


def logit_rows(value):
    high, middle, low = (part.astype(f32) for part in split_logits(value))
    row = lax.broadcasted_iota(jnp.int32, (ML, 128), 0)
    return jnp.where(row == 0, high, jnp.where(row == 1, middle, jnp.where(row == 2, low, 0.0)))


def slice_scratch():
    return [
        pltpu.VMEM((2, N, N, RP, QC), bf16),
        pltpu.VMEM((RC, N * N * QC), bf16),
        pltpu.VMEM((KR, N * N * KC), bf16),
        pltpu.VMEM((1, 32), f32),
        pltpu.SemaphoreType.DMA((2 * N + 5,)),
    ]


N_SCRATCH = 5


def in_hbm(*arrays):
    return tuple(pltpu.with_memory_space_constraint(a, pltpu.HBM) for a in arrays)


def in_hbm(*arrays):
    return tuple(pltpu.with_memory_space_constraint(a, pltpu.HBM) for a in arrays)


def total(*terms):
    value = terms[0].astype(f32)
    for term in terms[1:]:
        value = value + term.astype(f32)
    return value


def most(*terms):
    value = join_logits(terms[0])
    for term in terms[1:]:
        value = jnp.maximum(value, join_logits(term))
    return logit_rows(value)


C_PIECES = ((0, RC, 3, 0, QC), (1, KR, 2, 3 * RC, KC))


def sum_blocks(work, other, lanes, p, m, c):
    (core, main, rest), (blocks, c_query, c_key, own_logits, _) = work
    for copy in rest:
        copy.wait()
    lanes[pl.ds(0, 1), pl.ds(0, 32)] = own_logits[...]
    peak = jnp.maximum(lanes[pl.ds(0, 1), :], join_logits(other[0, 0, pl.ds(M_ALL, ML), :]))
    logit_block = logit_rows(peak).astype(bf16)

    @pl.loop(0, N * N)
    def _(i):
        at = (i // N, i % N)
        c[at + (pl.ds(MC, ML),)] = logit_block
        for source, height, width, start, size in C_PIECES:
            for lane in range(width):
                rows = start + lane * height
                c[at + (pl.ds(rows, height),)] = total(
                    (c_query, c_key)[source][:, columns(at[0], at[1], size, lane)],
                    other[at + (pl.ds(2 * MP + rows, height),)],
                ).astype(bf16)

    for i in range(N):
        main[2 * i].wait()
        main[2 * i + 1].wait()

        @pl.loop(0, N)
        def _(j):
            first, second = jnp.where(core == 0, j, i), jnp.where(core == 0, i, j)
            for owner, to in ((0, p), (1, m)):
                block = blocks[owner, i, j]
                for lane in range(3):
                    to[first, second, pl.ds(lane * RP, RP), :] = total(
                        block[:, lane * 128 : (lane + 1) * 128],
                        other[first, second, pl.ds(owner * MP + lane * RP, RP), :],
                    ).astype(bf16)


def collect_blocks(work, lanes, to):
    (core, main, rest), (blocks, c_query, c_key, own_logits, _) = work
    for copy in rest:
        copy.wait()
    lanes[pl.ds(0, 1), pl.ds(0, 32)] = own_logits[...]
    logit_block = logit_rows(lanes[pl.ds(0, 1), :]).astype(bf16)

    @pl.loop(0, N * N)
    def _(i):
        at = (i // N, i % N)
        to[at + (pl.ds(M_ALL, ML),)] = logit_block
        for source, height, width, start, size in C_PIECES:
            for lane in range(width):
                to[at + (pl.ds(2 * MP + start + lane * height, height),)] = (c_query, c_key)[
                    source
                ][:, columns(at[0], at[1], size, lane)]

    for i in range(N):
        main[2 * i].wait()
        main[2 * i + 1].wait()

        @pl.loop(0, N)
        def _(j):
            first, second = jnp.where(core == 0, j, i), jnp.where(core == 0, i, j)
            for owner in range(2):
                block = blocks[owner, i, j]
                for lane in range(3):
                    to[first, second, pl.ds(owner * MP + lane * RP, RP), :] = block[
                        :, lane * 128 : (lane + 1) * 128
                    ]


def local_kernel(sum_step, send_step, where, query, key, logits, *refs):
    refs = list(refs)
    other = [refs.pop(0)] if sum_step else []
    sums = [refs.pop(0) for _ in range(3)] if sum_step else []
    to = [refs.pop(0)] if send_step else []
    lanes = refs.pop()
    works = []
    for step, is_other in ((sum_step, False), (send_step, True)):
        if step:
            scratch, refs = refs[:N_SCRATCH], refs[N_SCRATCH:]
            copies = slice_copies(where, is_other, step, query, key, logits, scratch)
            for copy in copies[2] + copies[1]:
                copy.start()
            works.append((copies, scratch))
    lanes[...] = jnp.zeros_like(lanes)
    if sum_step:
        sum_blocks(works[0], *other, lanes, *sums)
    if send_step:
        collect_blocks(works[-1], lanes, *to)


def local(sum_step, send_step, where, query, key, logits, other=None):
    shapes, scratch, inputs = [], [], list(in_hbm(query, key, logits))
    if sum_step:
        shapes += [out((N, N, height, 128), bf16) for height in (MP, MP, MC + ML)]
        scratch += slice_scratch()
        inputs.append(other)
    if send_step:
        shapes += [out((N, N, M_ALL + ML, 128), bf16)]
        scratch += slice_scratch()
    return pl.pallas_call(
        functools.partial(local_kernel, sum_step, send_step),
        out_shape=shapes,
        in_specs=[SMEM, HBM, HBM, HBM] + [VMEM] * (1 if sum_step else 0),
        out_specs=[VMEM] * len(shapes),
        scratch_shapes=scratch + [pltpu.VMEM((8, 128), f32)],
        compiler_params=params(15 if sum_step and send_step else 10 if sum_step else 7),
        name=f"local_sum_{sum_step}_send_{send_step}",
    )(where, *inputs)


def add(first, second):
    return (first.astype(f32) + second.astype(f32)).astype(bf16)


def add_c_kernel(first, second, to):
    peak = most(first[0, 0, pl.ds(MC, ML), :], second[0, 0, pl.ds(MC, ML), :]).astype(bf16)

    @pl.loop(0, N * N)
    def _(i):
        rows = (i // N, i % N, pl.ds(0, MC))
        to[rows] = total(first[rows], second[rows]).astype(bf16)
        to[i // N, i % N, pl.ds(MC, ML), :] = peak


def add_c(first, second):
    return pl.pallas_call(
        add_c_kernel,
        out_shape=out((N, N, MC + ML, 128), bf16),
        in_specs=[VMEM, VMEM],
        out_specs=VMEM,
        compiler_params=params(6),
        name="add_c",
    )(first, second)


def split_ab_kernel(where, p0, m0, p1, m1, *outs):
    _, x, y, core = read(where)
    here = jnp.where(core == 0, y, x)
    for by, to in enumerate(outs):
        block = (here + by) % N

        @pl.loop(0, N)
        def _(i):
            to[i, pl.ds(0, MP), :] = total(p0[block, i], p1[block, i]).astype(bf16)
            to[i, pl.ds(MP, MP), :] = total(m0[block, i], m1[block, i]).astype(bf16)


def split_ab(where, own, received):
    return pl.pallas_call(
        split_ab_kernel,
        out_shape=[out((N, 2 * MP, 128), bf16)] * N,
        in_specs=[SMEM] + [VMEM] * 4,
        out_specs=[VMEM] * N,
        compiler_params=params(10),
        name="split_ab",
    )(where, *own, *received)


def split_c_kernel(where, c0, c1, *outs):
    peak = most(c0[0, 0, pl.ds(MC, ML), :], c1[0, 0, pl.ds(MC, ML), :]).astype(bf16)
    for by, to in enumerate(outs):
        block = (where[0] + by) % N

        @pl.loop(0, N)
        def _(i):
            rows = (block, i, pl.ds(0, MC))
            to[i, pl.ds(0, MC), :] = total(c0[rows], c1[rows]).astype(bf16)
            to[i, pl.ds(MC, ML), :] = peak


def split_c(where, own, received):
    return pl.pallas_call(
        split_c_kernel,
        out_shape=[out((N, MC + ML, 128), bf16)] * N,
        in_specs=[SMEM] + [VMEM] * 2,
        out_specs=[VMEM] * N,
        compiler_params=params(6),
        name="split_c",
    )(where, own, received)


def next_ab_kernel(where, t0, t1, t2, t3, *outs):
    z, _, y, core = read(where)
    here = jnp.where(core == 0, z, y)
    for by, to in enumerate(outs):
        block = (here + by) % N
        to[...] = total(t0[block], t1[block], t2[block], t3[block]).astype(bf16)


def next_c_kernel(where, t0, t1, t2, t3, *outs):
    terms = (t0, t1, t2, t3)
    peak = most(*(t[0, pl.ds(MC, ML), :] for t in terms)).astype(bf16)
    for by, to in enumerate(outs):
        rows = ((where[1] + by) % N, pl.ds(0, MC))
        to[pl.ds(0, MC), :] = total(*(t[rows] for t in terms)).astype(bf16)
        to[pl.ds(MC, ML), :] = peak


def next_parts(kernel, name, where, terms):
    return pl.pallas_call(
        kernel,
        out_shape=[out((terms[0].shape[1], 128), bf16)] * N,
        in_specs=[SMEM] + [VMEM] * N,
        out_specs=[VMEM] * N,
        compiler_params=params(6),
        name=name,
    )(where, *terms)


def scatter(blocks, axes):
    return [blocks[0]] + [shift(blocks[by], axes, (by, by)) for by in (1, 2, 3)]


def moment_kernel(
    where, a0, a1, a2, a3, c0, c1, c2, c3, qm, theirs, km, qm_out, km_out, gram0, gram1, peak
):
    core = where[3]
    part = total(a0[...], a1[...], a2[...], a3[...])
    rows = pl.ds(0, MC)
    part_c = total(c0[rows, :], c1[rows, :], c2[rows, :], c3[rows, :])
    rows = pl.ds(MC, ML)
    value = join_logits(c0[rows, :])
    for ref in (c1, c2, c3):
        value = jnp.maximum(value, join_logits(ref[rows, :]))
    peak[...] = jnp.broadcast_to(value, (8, 128))
    for lane in range(3):
        lanes = pl.ds(lane * 128, 128)
        for owner in range(2):
            rows = pl.ds(owner * RP, RP)
            start = owner * MP + lane * RP
            moment = jnp.where(core == owner, qm[rows, lanes], theirs[:, lanes])
            qm_out[rows, lanes] = momentum_decay * moment + part[start : start + RP]
        rows = pl.ds(2 * RP, RC)
        qm_out[rows, lanes] = (
            momentum_decay * qm[rows, lanes] + part_c[lane * RC : (lane + 1) * RC]
        )
    for lane in range(2):
        lanes = pl.ds(lane * 128, 128)
        start = 3 * RC + lane * KR
        km_out[:, lanes] = momentum_decay * km[:, lanes] + part_c[start : start + KR]

    def gram_of(value):
        return lax.dot_general(
            value, value, (((0,), (0,)), ((), ())), precision=HIGHEST, preferred_element_type=f32
        )

    full = qm_out[...]
    for head, to in enumerate((gram0, gram1)):
        wide = (full if head == 0 else pltpu.roll(full, QH, 1))[:, :256]
        gram = gram_of(wide)
        to[pl.ds(0, 192), :] = gram[:192, :128]
        to[pl.ds(192, 64), :] = gram[128:192, 128:]
        to[pl.ds(256, 128), :] = gram_of(km_out[:, pl.ds(head * KH, KH)])


def moments(where, part, part_c, query_moment, theirs, key_moment):
    return pl.pallas_call(
        moment_kernel,
        out_shape=(
            out((QR, QC), f32),
            out((KR, KC), f32),
            out((G_ROWS, 128), f32),
            out((G_ROWS, 128), f32),
            out((8, 128), f32),
        ),
        in_specs=[SMEM] + [VMEM] * 11,
        out_specs=(VMEM,) * 5,
        compiler_params=params(12),
        name="moments",
    )(where, *part, *part_c, query_moment, theirs, key_moment)


def three_products(left, right):
    def halves(value):
        high = value.astype(bf16)
        return high, (value - high.astype(f32)).astype(bf16)

    def product(first, second):
        return jnp.dot(first, second, preferred_element_type=f32)

    (left_high, left_low), (right_high, right_low) = halves(left), halves(right)
    return product(left_high, right_high) + (
        product(left_high, right_low) + product(left_low, right_high)
    )


def chain_kernel(g0, g1, g2, g3, to):
    packed = g0[...] + g1[...] + g2[...] + g3[...]
    top, side, corner = packed[:128], packed[128:192], packed[192:256]
    key_gram = packed[256:384]
    row = lax.broadcasted_iota(jnp.int32, (256, 256), 0)
    column = lax.broadcasted_iota(jnp.int32, (256, 256), 1)
    zeros = jnp.zeros((64, 128), f32)
    lower = jnp.concatenate([side, zeros], axis=0)
    query_gram = jnp.concatenate(
        [
            jnp.concatenate([top, lower.T], axis=1),
            jnp.concatenate([lower, jnp.concatenate([corner, zeros], axis=0)], axis=1),
        ],
        axis=0,
    )
    query_gram = jnp.where((row < QH) & (column < QH), query_gram, 0.0)
    query_eye = jnp.where((row == column) & (row < QH), 1.0, 0.0).astype(f32)
    key_eye = jnp.where(row == column, 1.0, 0.0).astype(f32)[:128, :128]

    def product(left, right, exact):
        if exact:
            return jnp.dot(left, right, precision=HIGHEST, preferred_element_type=f32)
        return three_products(left, right)

    def start(gram, eye):
        square = jnp.sum(jnp.sum(gram * eye, axis=1, keepdims=True), axis=0, keepdims=True)
        inverse = 1.0 / (jnp.sqrt(square) + norm_epsilon)
        return gram * inverse * inverse, inverse

    grams, inverses = zip(start(query_gram, query_eye), start(key_gram, key_eye))
    grams, eyes, totals = list(grams), (query_eye, key_eye), [None, None]
    for iteration in range(ITERS):
        exact = iteration < 2
        mixers = []
        for i in range(2):
            square = product(grams[i], grams[i], exact)
            mixers.append(coef_first * eyes[i] + coef_second * grams[i] + coef_third * square)
        if iteration < ITERS - 1:
            halves = [product(mixers[i], grams[i], exact) for i in range(2)]
        for i in range(2):
            totals[i] = mixers[i] if iteration == 0 else product(totals[i], mixers[i], exact)
        if iteration < ITERS - 1:
            grams = [product(halves[i], mixers[i], exact) for i in range(2)]
    query_total, key_total = (totals[i] * inverses[i] for i in range(2))
    to[pl.ds(0, 192), :] = query_total[:192, :128]
    to[pl.ds(192, 192), :] = query_total[:192, 128:]
    to[pl.ds(384, 128), :] = key_total


def chain(grams):
    return pl.pallas_call(
        chain_kernel,
        out_shape=out((512, 128), f32),
        in_specs=[VMEM] * 4,
        out_specs=VMEM,
        compiler_params=params(12),
        name="newton_schulz_polynomial",
    )(*grams)

def update_kernel(where, own, other, peak, qm, km, qw, kw, to):
    z, x, _, core = read(where)
    mine, theirs = own[...], other[...]
    packs = (jnp.where(core == 0, mine, theirs), jnp.where(core == 0, theirs, mine))

    product = three_products
    gamma = jnp.minimum(1.0, clip_limit / peak[pl.ds(0, 1), :])
    lane = lax.broadcasted_iota(jnp.int32, (1, 128), 1)
    first_head = 2 * (z * N + x)
    gammas = [
        jnp.sum(jnp.where(lane == first_head + h, gamma, 0.0), axis=1, keepdims=True)
        for h in range(2)
    ]
    roots = [jnp.sqrt(g) for g in gammas]
    column = lax.broadcasted_iota(jnp.int32, (1, QC), 1)
    second = column >= QH
    rope = jnp.where(second, column - QH, column) >= QH - QROPE
    query_factor = jnp.where(
        rope, jnp.where(second, gammas[1], gammas[0]), jnp.where(second, roots[1], roots[0])
    )
    key_factor = jnp.where(
        lax.broadcasted_iota(jnp.int32, (1, KC), 1) >= KH, roots[1], roots[0]
    )

    full = qm[...]
    zeros = jnp.zeros((64, 256), f32)
    pad = jnp.zeros((QR, 128), f32)
    pieces = []
    for head in range(2):
        wide = (full if head == 0 else pltpu.roll(full, QH, 1))[:, :256]
        matrix = jnp.concatenate([packs[head][:192], packs[head][192:384]], axis=1)
        matrix = jnp.concatenate([matrix, zeros], axis=0)
        piece = jnp.concatenate([product(wide, matrix), pad], axis=1)
        pieces.append(piece if head == 0 else pltpu.roll(piece, QH, 1))
    query_ortho = pieces[0] + pieces[1]
    key_ortho = jnp.concatenate(
        [product(km[:, pl.ds(h * KH, KH)], packs[h][384:]) for h in range(2)], axis=1
    )
    query_scale = 0.2 * math.sqrt(max(QL, QH))
    key_scale = 0.2 * math.sqrt(max(KVL, KH))
    query_weight, key_weight = qw[...], kw[...]
    query_next = query_weight - learn_rate * (
        query_scale * query_ortho + weight_decay * query_weight
    )
    key_next = key_weight - learn_rate * (key_scale * key_ortho + weight_decay * key_weight)
    query_block = (query_next * query_factor).astype(bf16)
    key_block = (key_next * key_factor).astype(bf16)
    half = QR // 2
    for i in range(2):
        start = i * M_HALF
        to[pl.ds(start, QR), :] = query_block[:, i * 128 : (i + 1) * 128]
        to[pl.ds(start + QR, half), :] = query_block[i * half : (i + 1) * half, 256:]
        to[pl.ds(start + QR + half, KR), :] = key_block[:, i * 128 : (i + 1) * 128]


def update(where, own, other, peak, query_moment, key_moment, query_weight, key_weight):
    return pl.pallas_call(
        update_kernel,
        out_shape=out((M_ALL, 128), bf16),
        in_specs=[SMEM] + [VMEM] * 7,
        out_specs=VMEM,
        compiler_params=params(12),
        name="update",
    )(where, own, other, peak, query_moment, key_moment, query_weight, key_weight)


def assemble_kernel(where, *refs):
    z, x, _, core = read(where)
    stacks, (query_out, key_out) = (refs[:N], refs[N : 2 * N]), refs[2 * N :]
    half = QR // 2
    for far in range(N):

        @pl.loop(0, N)
        def _(near):
            back_z = jnp.where(core == 0, near, far)
            back_x = jnp.where(core == 0, far, near)
            zz, xx = (z + N - back_z) % N, (x + N - back_x) % N
            for i in range(2):
                stack = stacks[i][far]
                query_out[:, columns(zz, xx, QC, i)] = stack[near, pl.ds(0, QR), :]
                query_out[pl.ds(i * half, half), columns(zz, xx, QC, 2)] = stack[
                    near, pl.ds(QR, half), :
                ]
                key_out[:, columns(zz, xx, KC, i)] = stack[near, pl.ds(QR + half, KR), :]


def assemble(where, first, second):
    return pl.pallas_call(
        assemble_kernel,
        out_shape=(out((QR, N * N * QC), bf16), out((KR, N * N * KC), bf16)),
        in_specs=[SMEM] + [VMEM] * (2 * N),
        out_specs=(VMEM, VMEM),
        compiler_params=params(16),
        name="assemble",
    )(where, *first, *second)


def on_device(grad_query, grad_key, query_weight, key_weight, query_moment, key_moment, max_logits):
    dp, ctx = lax.axis_index("dp"), lax.axis_index("ctx")
    z, x, y, core = dp // N, dp % N, ctx // 2, ctx % 2
    where = jnp.stack([z, x, y, core]).astype(jnp.int32)
    query = grad_query.reshape(N, 2, QR, N * N * QC)
    key = grad_key.reshape(N, 2, KR, N * N * KC)

    def after(value):
        return lax.optimization_barrier((where, value))[0]

    others, token = [], where
    for step in range(1, N):
        (blocks,) = local(None, step, token, query, key, max_logits)
        token = after(blocks)
        others.append(swap(blocks))
    pre = [local(1, None, where, query, key, max_logits, others[0])]
    *sums, blocks = local(2, N, after(pre[0][0]), query, key, max_logits, others[1])
    pre.append(sums)
    others.append(swap(blocks))
    for step in range(3, N + 1):
        pre.append(local(step, None, where, query, key, max_logits, others[step - 1]))

    p, m, c = pre[0]
    for step in range(1, N):
        p = shift(p, ("x", "z"), (1, 1))
        m = shift(m, ("x", "z"), (-1, -1))
        c = shift(c, ("y", "y"), (1, -1))
        if step < N - 1:
            p, m, c = add(pre[step][0], p), add(pre[step][1], m), add_c(pre[step][2], c)
        if step == 1:
            theirs = swap(lax.dynamic_slice_in_dim(query_moment, (1 - after(c)[3]) * RP, RP, 0))
    pre = pre[-1]

    part = split_ab(where, pre[:2], (p, m))
    part_c = split_c(after(part[0]), pre[2], c)
    part, part_c = scatter(part, ("y", "x")), scatter(part_c, ("z", "z"))
    part = next_parts(next_ab_kernel, "next_ab", where, part)
    part_c = next_parts(next_c_kernel, "next_c", after(part[0]), part_c)
    part, part_c = scatter(part, ("z", "y")), scatter(part_c, ("x", "x"))
    moment, new_key_moment, gram0, gram1, peak = moments(
        where, part, part_c, query_moment, theirs, key_moment
    )

    keep, give = jnp.where(core == 0, gram0, gram1), jnp.where(core == 0, gram1, gram0)
    gram = keep + swap(give)
    own = chain([gram] + [shift(gram, ("y", "y"), (by, by)) for by in (1, 2, 3)])

    theirs = swap(lax.dynamic_slice_in_dim(moment, (1 - core) * RP, RP, 0))
    new_query_moment = jnp.concatenate(
        [
            jnp.where(core == 0, moment[:RP], theirs),
            jnp.where(core == 0, theirs, moment[RP : 2 * RP]),
            moment[2 * RP :],
        ]
    )
    block = update(
        where, own, swap(own), peak, new_query_moment, new_key_moment, query_weight, key_weight
    )
    blocks = [block] + [shift(block, ("z", "x"), (by, by)) for by in (1, 2, 3)]

    def along(stack, by):
        return shift(stack, ("x", "z"), (by, by))

    first, second = (jnp.stack([b[i * M_HALF : (i + 1) * M_HALF] for b in blocks]) for i in range(2))
    first_back, second_ahead = along(first, 1), along(second, -1)
    second_back, first_ahead = along(second, 1), along(first, -1)
    first_far, second_far = along(first_back, 1), along(second_ahead, -1)
    query_out, key_out = assemble(
        where,
        (first, first_back, first_far, first_ahead),
        (second, second_back, second_far, second_ahead),
    )
    return (query_out, key_out, new_query_moment, new_key_moment)


def solution(mesh):
    in_specs = (
        P(("dp", "ctx"), None, None),
        P(("dp", "ctx"), None, None),
        P("ctx", "dp"),
        P("ctx", "dp"),
        P("ctx", "dp"),
        P("ctx", "dp"),
        P(("dp", "ctx"), None),
    )
    out_specs = (P("ctx", None), P("ctx", None), P("ctx", "dp"), P("ctx", "dp"))
    return jax.shard_map(
        on_device, mesh=mesh, in_specs=in_specs, out_specs=out_specs, check_vma=False
    )
```

```python
import functools
import math

import jax
import jax.numpy as jnp
from jax import lax
from jax.experimental import pallas as pl
from jax.experimental.pallas import tpu as pltpu
from jax.sharding import PartitionSpec as P

QL = 1536
KVL = 512
QH = 192
QROPE = 64
KH = 128
ITERS = 5

momentum_decay = 0.9
learn_rate = 0.2
weight_decay = 0.1
clip_limit = 100.0
norm_epsilon = 1e-07
coef_first = 3.4445
coef_second = -4.775
coef_third = 2.0315

N = 4
QC, KC = 384, 256
QR, KR = 192, 64
RP, RC = 80, 32
MP = RP * 3
MC = RC * 3 + KR * 2
ML = 16
M_ALL = 2 * MP + MC
M_HALF = M_ALL // 2
G_ROWS = 288

f32, bf16 = jnp.float32, jnp.bfloat16
AXES = ("dp", "ctx")
VMEM = pl.BlockSpec(memory_space=pltpu.VMEM)
SMEM = pl.BlockSpec(memory_space=pltpu.SMEM)
HBM = pl.BlockSpec(memory_space=pltpu.HBM)
HIGHEST = lax.Precision.HIGHEST


def params(mib):
    return pltpu.CompilerParams(vmem_limit_bytes=mib << 20)


def out(shape, dtype):
    return jax.ShapeDtypeStruct(shape, dtype)


def place(z, x, y, c):
    return ((z % N) * N + x % N) * 2 * N + (y % N) * 2 + c


def shift(array, axes, steps):
    def target(z, x, y, c):
        axis, by = axes[c], steps[c]
        return (z + by * (axis == "z"), x + by * (axis == "x"), y + by * (axis == "y"), c)

    pairs = [
        (place(z, x, y, c), place(*target(z, x, y, c)))
        for z in range(N)
        for x in range(N)
        for y in range(N)
        for c in range(2)
    ]
    return lax.ppermute(array, AXES, pairs)


def swap(array):
    pairs = [(i, i ^ 1) for i in range(2 * N**3)]
    return lax.ppermute(array, AXES, pairs)


def read(where):
    return where[0], where[1], where[2], where[3]


def columns(zz, xx, width, lane=None):
    start = (zz * N + xx) * width
    if lane is None:
        return pl.ds(pl.multiple_of(start, 128), width)
    return pl.ds(pl.multiple_of(start + lane * 128, 128), 128)


def slice_copies(where, other, step, query, key, logits, scratch):
    blocks, c_query, c_key, own_logits, sems = scratch
    z, x, y, core = read(where)
    if other:
        core = 1 - core
    ahead = N - step
    here = jnp.where(core == 0, x, z) + N
    block_c = (y + (1 - 2 * core) * ahead + N) % N
    main = []
    for i in range(N):
        for owner, block in ((0, (here + ahead) % N), (1, (here - ahead) % N)):
            start = jnp.where(core == 0, i * N + block, block * N + i) * QC
            main.append(
                pltpu.make_async_copy(
                    query.at[
                        :,
                        owner,
                        pl.ds(pl.multiple_of(core * RP, 16), RP),
                        pl.ds(pl.multiple_of(start, 128), QC),
                    ],
                    blocks.at[owner, i],
                    sems.at[owner * N + i],
                )
            )
    rest = [pltpu.make_async_copy(logits, own_logits, sems.at[2 * N])]
    for half in range(2):
        rows = pl.ds(half * RC // 2, RC // 2)
        rest.append(
            pltpu.make_async_copy(
                query.at[block_c, core, pl.ds(2 * RP + half * RC // 2, RC // 2), :],
                c_query.at[rows, :],
                sems.at[2 * N + 1 + 2 * half],
            )
        )
        rows = pl.ds(half * KR // 2, KR // 2)
        rest.append(
            pltpu.make_async_copy(
                key.at[block_c, core, rows, :],
                c_key.at[rows, :],
                sems.at[2 * N + 2 + 2 * half],
            )
        )
    return core, main, rest


def split_logits(value):
    high = value.astype(bf16)
    rest = value - high.astype(f32)
    middle = rest.astype(bf16)
    low = (rest - middle.astype(f32)).astype(bf16)
    return high, middle, low


def join_logits(rows):
    rows = rows.astype(f32)
    return rows[0:1] + rows[1:2] + rows[2:3]


def logit_rows(value):
    high, middle, low = (part.astype(f32) for part in split_logits(value))
    row = lax.broadcasted_iota(jnp.int32, (ML, 128), 0)
    return jnp.where(row == 0, high, jnp.where(row == 1, middle, jnp.where(row == 2, low, 0.0)))


def slice_scratch():
    return [
        pltpu.VMEM((2, N, N, RP, QC), bf16),
        pltpu.VMEM((RC, N * N * QC), bf16),
        pltpu.VMEM((KR, N * N * KC), bf16),
        pltpu.VMEM((1, 32), f32),
        pltpu.SemaphoreType.DMA((2 * N + 5,)),
    ]


N_SCRATCH = 5


def in_hbm(*arrays):
    return tuple(pltpu.with_memory_space_constraint(a, pltpu.HBM) for a in arrays)


def in_hbm(*arrays):
    return tuple(pltpu.with_memory_space_constraint(a, pltpu.HBM) for a in arrays)


def total(*terms):
    value = terms[0].astype(f32)
    for term in terms[1:]:
        value = value + term.astype(f32)
    return value


def most(*terms):
    value = join_logits(terms[0])
    for term in terms[1:]:
        value = jnp.maximum(value, join_logits(term))
    return logit_rows(value)


C_PIECES = ((0, RC, 3, 0, QC), (1, KR, 2, 3 * RC, KC))


def sum_blocks(work, other, lanes, p, m, c):
    (core, main, rest), (blocks, c_query, c_key, own_logits, _) = work
    for copy in rest:
        copy.wait()
    lanes[pl.ds(0, 1), pl.ds(0, 32)] = own_logits[...]
    peak = jnp.maximum(lanes[pl.ds(0, 1), :], join_logits(other[0, 0, pl.ds(M_ALL, ML), :]))
    logit_block = logit_rows(peak).astype(bf16)

    @pl.loop(0, N * N)
    def _(i):
        at = (i // N, i % N)
        c[at + (pl.ds(MC, ML),)] = logit_block
        for source, height, width, start, size in C_PIECES:
            for lane in range(width):
                rows = start + lane * height
                c[at + (pl.ds(rows, height),)] = total(
                    (c_query, c_key)[source][:, columns(at[0], at[1], size, lane)],
                    other[at + (pl.ds(2 * MP + rows, height),)],
                ).astype(bf16)

    for i in range(N):
        main[2 * i].wait()
        main[2 * i + 1].wait()

        @pl.loop(0, N)
        def _(j):
            first, second = jnp.where(core == 0, j, i), jnp.where(core == 0, i, j)
            for owner, to in ((0, p), (1, m)):
                block = blocks[owner, i, j]
                for lane in range(3):
                    to[first, second, pl.ds(lane * RP, RP), :] = total(
                        block[:, lane * 128 : (lane + 1) * 128],
                        other[first, second, pl.ds(owner * MP + lane * RP, RP), :],
                    ).astype(bf16)


def collect_blocks(work, lanes, to):
    (core, main, rest), (blocks, c_query, c_key, own_logits, _) = work
    for copy in rest:
        copy.wait()
    lanes[pl.ds(0, 1), pl.ds(0, 32)] = own_logits[...]
    logit_block = logit_rows(lanes[pl.ds(0, 1), :]).astype(bf16)

    @pl.loop(0, N * N)
    def _(i):
        at = (i // N, i % N)
        to[at + (pl.ds(M_ALL, ML),)] = logit_block
        for source, height, width, start, size in C_PIECES:
            for lane in range(width):
                to[at + (pl.ds(2 * MP + start + lane * height, height),)] = (c_query, c_key)[
                    source
                ][:, columns(at[0], at[1], size, lane)]

    for i in range(N):
        main[2 * i].wait()
        main[2 * i + 1].wait()

        @pl.loop(0, N)
        def _(j):
            first, second = jnp.where(core == 0, j, i), jnp.where(core == 0, i, j)
            for owner in range(2):
                block = blocks[owner, i, j]
                for lane in range(3):
                    to[first, second, pl.ds(owner * MP + lane * RP, RP), :] = block[
                        :, lane * 128 : (lane + 1) * 128
                    ]


def local_kernel(sum_step, send_step, where, query, key, logits, *refs):
    refs = list(refs)
    other = [refs.pop(0)] if sum_step else []
    sums = [refs.pop(0) for _ in range(3)] if sum_step else []
    to = [refs.pop(0)] if send_step else []
    lanes = refs.pop()
    works = []
    for step, is_other in ((sum_step, False), (send_step, True)):
        if step:
            scratch, refs = refs[:N_SCRATCH], refs[N_SCRATCH:]
            copies = slice_copies(where, is_other, step, query, key, logits, scratch)
            for copy in copies[2] + copies[1]:
                copy.start()
            works.append((copies, scratch))
    lanes[...] = jnp.zeros_like(lanes)
    if sum_step:
        sum_blocks(works[0], *other, lanes, *sums)
    if send_step:
        collect_blocks(works[-1], lanes, *to)


def local(sum_step, send_step, where, query, key, logits, other=None):
    shapes, scratch, inputs = [], [], list(in_hbm(query, key, logits))
    if sum_step:
        shapes += [out((N, N, height, 128), bf16) for height in (MP, MP, MC + ML)]
        scratch += slice_scratch()
        inputs.append(other)
    if send_step:
        shapes += [out((N, N, M_ALL + ML, 128), bf16)]
        scratch += slice_scratch()
    return pl.pallas_call(
        functools.partial(local_kernel, sum_step, send_step),
        out_shape=shapes,
        in_specs=[SMEM, HBM, HBM, HBM] + [VMEM] * (1 if sum_step else 0),
        out_specs=[VMEM] * len(shapes),
        scratch_shapes=scratch + [pltpu.VMEM((8, 128), f32)],
        compiler_params=params(15 if sum_step and send_step else 10 if sum_step else 7),
        name=f"local_sum_{sum_step}_send_{send_step}",
    )(where, *inputs)


def add(first, second):
    return (first.astype(f32) + second.astype(f32)).astype(bf16)


def add_c_kernel(first, second, to):
    peak = most(first[0, 0, pl.ds(MC, ML), :], second[0, 0, pl.ds(MC, ML), :]).astype(bf16)

    @pl.loop(0, N * N)
    def _(i):
        rows = (i // N, i % N, pl.ds(0, MC))
        to[rows] = total(first[rows], second[rows]).astype(bf16)
        to[i // N, i % N, pl.ds(MC, ML), :] = peak


def add_c(first, second):
    return pl.pallas_call(
        add_c_kernel,
        out_shape=out((N, N, MC + ML, 128), bf16),
        in_specs=[VMEM, VMEM],
        out_specs=VMEM,
        compiler_params=params(6),
        name="add_c",
    )(first, second)


def split_ab_kernel(where, p0, m0, p1, m1, *outs):
    _, x, y, core = read(where)
    here = jnp.where(core == 0, y, x)
    for by, to in enumerate(outs):
        block = (here + by) % N

        @pl.loop(0, N)
        def _(i):
            to[i, pl.ds(0, MP), :] = total(p0[block, i], p1[block, i]).astype(bf16)
            to[i, pl.ds(MP, MP), :] = total(m0[block, i], m1[block, i]).astype(bf16)


def split_ab(where, own, received):
    return pl.pallas_call(
        split_ab_kernel,
        out_shape=[out((N, 2 * MP, 128), bf16)] * N,
        in_specs=[SMEM] + [VMEM] * 4,
        out_specs=[VMEM] * N,
        compiler_params=params(10),
        name="split_ab",
    )(where, *own, *received)


def split_c_kernel(where, c0, c1, *outs):
    peak = most(c0[0, 0, pl.ds(MC, ML), :], c1[0, 0, pl.ds(MC, ML), :]).astype(bf16)
    for by, to in enumerate(outs):
        block = (where[0] + by) % N

        @pl.loop(0, N)
        def _(i):
            rows = (block, i, pl.ds(0, MC))
            to[i, pl.ds(0, MC), :] = total(c0[rows], c1[rows]).astype(bf16)
            to[i, pl.ds(MC, ML), :] = peak


def split_c(where, own, received):
    return pl.pallas_call(
        split_c_kernel,
        out_shape=[out((N, MC + ML, 128), bf16)] * N,
        in_specs=[SMEM] + [VMEM] * 2,
        out_specs=[VMEM] * N,
        compiler_params=params(6),
        name="split_c",
    )(where, own, received)


def next_ab_kernel(where, t0, t1, t2, t3, *outs):
    z, _, y, core = read(where)
    here = jnp.where(core == 0, z, y)
    for by, to in enumerate(outs):
        block = (here + by) % N
        to[...] = total(t0[block], t1[block], t2[block], t3[block]).astype(bf16)


def next_c_kernel(where, t0, t1, t2, t3, *outs):
    terms = (t0, t1, t2, t3)
    peak = most(*(t[0, pl.ds(MC, ML), :] for t in terms)).astype(bf16)
    for by, to in enumerate(outs):
        rows = ((where[1] + by) % N, pl.ds(0, MC))
        to[pl.ds(0, MC), :] = total(*(t[rows] for t in terms)).astype(bf16)
        to[pl.ds(MC, ML), :] = peak


def next_parts(kernel, name, where, terms):
    return pl.pallas_call(
        kernel,
        out_shape=[out((terms[0].shape[1], 128), bf16)] * N,
        in_specs=[SMEM] + [VMEM] * N,
        out_specs=[VMEM] * N,
        compiler_params=params(6),
        name=name,
    )(where, *terms)


def scatter(blocks, axes):
    return [blocks[0]] + [shift(blocks[by], axes, (by, by)) for by in (1, 2, 3)]


def moment_kernel(
    where, a0, a1, a2, a3, c0, c1, c2, c3, qm, theirs, km, qm_out, km_out, gram0, gram1, peak
):
    core = where[3]
    part = total(a0[...], a1[...], a2[...], a3[...])
    rows = pl.ds(0, MC)
    part_c = total(c0[rows, :], c1[rows, :], c2[rows, :], c3[rows, :])
    rows = pl.ds(MC, ML)
    value = join_logits(c0[rows, :])
    for ref in (c1, c2, c3):
        value = jnp.maximum(value, join_logits(ref[rows, :]))
    peak[...] = jnp.broadcast_to(value, (8, 128))
    for lane in range(3):
        lanes = pl.ds(lane * 128, 128)
        for owner in range(2):
            rows = pl.ds(owner * RP, RP)
            start = owner * MP + lane * RP
            moment = jnp.where(core == owner, qm[rows, lanes], theirs[:, lanes])
            qm_out[rows, lanes] = momentum_decay * moment + part[start : start + RP]
        rows = pl.ds(2 * RP, RC)
        qm_out[rows, lanes] = (
            momentum_decay * qm[rows, lanes] + part_c[lane * RC : (lane + 1) * RC]
        )
    for lane in range(2):
        lanes = pl.ds(lane * 128, 128)
        start = 3 * RC + lane * KR
        km_out[:, lanes] = momentum_decay * km[:, lanes] + part_c[start : start + KR]

    def gram_of(value):
        return lax.dot_general(
            value, value, (((0,), (0,)), ((), ())), precision=HIGHEST, preferred_element_type=f32
        )

    full = qm_out[...]
    for head, to in enumerate((gram0, gram1)):
        wide = (full if head == 0 else pltpu.roll(full, QH, 1))[:, :256]
        gram = gram_of(wide)
        left = lax.broadcasted_iota(jnp.int32, (64, 128), 1) < 64
        to[pl.ds(0, 64), :] = jnp.where(
            left, gram[:64, :128], pltpu.roll(gram[128:192, 128:], 64, 1)
        )
        to[pl.ds(64, 128), :] = gram[64:192, :128]
        gram = gram_of(km_out[:, pl.ds(head * KH, KH)])
        to[pl.ds(192, 64), :] = gram[64:]
        to[pl.ds(256, 32), :] = jnp.where(left[:32], gram[:32], pltpu.roll(gram[32:64], 64, 1))


def moments(where, part, part_c, query_moment, theirs, key_moment):
    return pl.pallas_call(
        moment_kernel,
        out_shape=(
            out((QR, QC), f32),
            out((KR, KC), f32),
            out((G_ROWS, 128), f32),
            out((G_ROWS, 128), f32),
            out((8, 128), f32),
        ),
        in_specs=[SMEM] + [VMEM] * 11,
        out_specs=(VMEM,) * 5,
        compiler_params=params(12),
        name="moments",
    )(where, *part, *part_c, query_moment, theirs, key_moment)


def three_products(left, right):
    def halves(value):
        high = value.astype(bf16)
        return high, (value - high.astype(f32)).astype(bf16)

    def product(first, second):
        return jnp.dot(first, second, preferred_element_type=f32)

    (left_high, left_low), (right_high, right_low) = halves(left), halves(right)
    return product(left_high, right_high) + (
        product(left_high, right_low) + product(left_low, right_high)
    )


def chain_kernel(g0, g1, g2, g3, to):
    packed = g0[...] + g1[...] + g2[...] + g3[...]
    row = lax.broadcasted_iota(jnp.int32, (256, 256), 0)
    column = lax.broadcasted_iota(jnp.int32, (256, 256), 1)
    left = lax.broadcasted_iota(jnp.int32, (64, 128), 1) < 64
    zeros = jnp.zeros((64, 128), f32)

    def stacked(*blocks):
        return jnp.concatenate(blocks, axis=0)

    def part(block, keep_left):
        return jnp.where(left if keep_left else ~left, block, 0.0)

    diagonal, middle, last = packed[:64], packed[64:128], packed[128:192]
    lower = stacked(zeros, part(middle, True), last, zeros)
    first = lower + stacked(part(diagonal, True), part(middle, False), zeros, zeros)
    corner = part(pltpu.roll(diagonal, 64, 1), True)
    query_gram = jnp.concatenate(
        [first, stacked(zeros, zeros, corner, zeros)], axis=1
    ) + stacked(lower.T, jnp.zeros((128, 256), f32))
    middle, diagonal = packed[192:256], packed[256:288]
    lower = stacked(zeros, part(middle, True))
    diagonal = part(stacked(diagonal, pltpu.roll(diagonal, 64, 1)), True)
    key_gram = lower + lower.T + stacked(diagonal, part(middle, False))
    query_eye = jnp.where((row == column) & (row < QH), 1.0, 0.0).astype(f32)
    key_eye = jnp.where(row == column, 1.0, 0.0).astype(f32)[:128, :128]

    def product(left, right, exact):
        if exact:
            return jnp.dot(left, right, precision=HIGHEST, preferred_element_type=f32)
        return three_products(left, right)

    def start(gram, eye):
        square = jnp.sum(jnp.sum(gram * eye, axis=1, keepdims=True), axis=0, keepdims=True)
        inverse = 1.0 / (jnp.sqrt(square) + norm_epsilon)
        return gram * inverse * inverse, inverse

    grams, inverses = zip(start(query_gram, query_eye), start(key_gram, key_eye))
    grams, eyes, totals = list(grams), (query_eye, key_eye), [None, None]
    for iteration in range(ITERS):
        exact = iteration < 2
        mixers = []
        for i in range(2):
            square = product(grams[i], grams[i], exact)
            mixers.append(coef_first * eyes[i] + coef_second * grams[i] + coef_third * square)
        if iteration < ITERS - 1:
            halves = [product(mixers[i], grams[i], exact) for i in range(2)]
        for i in range(2):
            totals[i] = mixers[i] if iteration == 0 else product(totals[i], mixers[i], exact)
        if iteration < ITERS - 1:
            grams = [product(halves[i], mixers[i], exact) for i in range(2)]
    query_total, key_total = (totals[i] * inverses[i] for i in range(2))
    to[pl.ds(0, 192), :] = query_total[:192, :128]
    to[pl.ds(192, 192), :] = query_total[:192, 128:]
    to[pl.ds(384, 128), :] = key_total


def chain(grams):
    return pl.pallas_call(
        chain_kernel,
        out_shape=out((512, 128), f32),
        in_specs=[VMEM] * 4,
        out_specs=VMEM,
        compiler_params=params(12),
        name="newton_schulz_polynomial",
    )(*grams)

def update_kernel(where, own, other, peak, qm, km, qw, kw, to):
    z, x, _, core = read(where)
    mine, theirs = own[...], other[...]
    packs = (jnp.where(core == 0, mine, theirs), jnp.where(core == 0, theirs, mine))

    product = three_products
    gamma = jnp.minimum(1.0, clip_limit / peak[pl.ds(0, 1), :])
    lane = lax.broadcasted_iota(jnp.int32, (1, 128), 1)
    first_head = 2 * (z * N + x)
    gammas = [
        jnp.sum(jnp.where(lane == first_head + h, gamma, 0.0), axis=1, keepdims=True)
        for h in range(2)
    ]
    roots = [jnp.sqrt(g) for g in gammas]
    column = lax.broadcasted_iota(jnp.int32, (1, QC), 1)
    second = column >= QH
    rope = jnp.where(second, column - QH, column) >= QH - QROPE
    query_factor = jnp.where(
        rope, jnp.where(second, gammas[1], gammas[0]), jnp.where(second, roots[1], roots[0])
    )
    key_factor = jnp.where(
        lax.broadcasted_iota(jnp.int32, (1, KC), 1) >= KH, roots[1], roots[0]
    )

    full = qm[...]
    zeros = jnp.zeros((64, 256), f32)
    pad = jnp.zeros((QR, 128), f32)
    pieces = []
    for head in range(2):
        wide = (full if head == 0 else pltpu.roll(full, QH, 1))[:, :256]
        matrix = jnp.concatenate([packs[head][:192], packs[head][192:384]], axis=1)
        matrix = jnp.concatenate([matrix, zeros], axis=0)
        piece = jnp.concatenate([product(wide, matrix), pad], axis=1)
        pieces.append(piece if head == 0 else pltpu.roll(piece, QH, 1))
    query_ortho = pieces[0] + pieces[1]
    key_ortho = jnp.concatenate(
        [product(km[:, pl.ds(h * KH, KH)], packs[h][384:]) for h in range(2)], axis=1
    )
    query_scale = 0.2 * math.sqrt(max(QL, QH))
    key_scale = 0.2 * math.sqrt(max(KVL, KH))
    query_weight, key_weight = qw[...], kw[...]
    query_next = query_weight - learn_rate * (
        query_scale * query_ortho + weight_decay * query_weight
    )
    key_next = key_weight - learn_rate * (key_scale * key_ortho + weight_decay * key_weight)
    query_block = (query_next * query_factor).astype(bf16)
    key_block = (key_next * key_factor).astype(bf16)
    half = QR // 2
    for i in range(2):
        start = i * M_HALF
        to[pl.ds(start, QR), :] = query_block[:, i * 128 : (i + 1) * 128]
        to[pl.ds(start + QR, half), :] = query_block[i * half : (i + 1) * half, 256:]
        to[pl.ds(start + QR + half, KR), :] = key_block[:, i * 128 : (i + 1) * 128]


def update(where, own, other, peak, query_moment, key_moment, query_weight, key_weight):
    return pl.pallas_call(
        update_kernel,
        out_shape=out((M_ALL, 128), bf16),
        in_specs=[SMEM] + [VMEM] * 7,
        out_specs=VMEM,
        compiler_params=params(12),
        name="update",
    )(where, own, other, peak, query_moment, key_moment, query_weight, key_weight)


def assemble_kernel(where, *refs):
    z, x, _, core = read(where)
    stacks, (query_out, key_out) = (refs[:N], refs[N : 2 * N]), refs[2 * N :]
    half = QR // 2
    for far in range(N):

        @pl.loop(0, N)
        def _(near):
            back_z = jnp.where(core == 0, near, far)
            back_x = jnp.where(core == 0, far, near)
            zz, xx = (z + N - back_z) % N, (x + N - back_x) % N
            for i in range(2):
                stack = stacks[i][far]
                query_out[:, columns(zz, xx, QC, i)] = stack[near, pl.ds(0, QR), :]
                query_out[pl.ds(i * half, half), columns(zz, xx, QC, 2)] = stack[
                    near, pl.ds(QR, half), :
                ]
                key_out[:, columns(zz, xx, KC, i)] = stack[near, pl.ds(QR + half, KR), :]


def assemble(where, first, second):
    return pl.pallas_call(
        assemble_kernel,
        out_shape=(out((QR, N * N * QC), bf16), out((KR, N * N * KC), bf16)),
        in_specs=[SMEM] + [VMEM] * (2 * N),
        out_specs=(VMEM, VMEM),
        compiler_params=params(16),
        name="assemble",
    )(where, *first, *second)


def on_device(grad_query, grad_key, query_weight, key_weight, query_moment, key_moment, max_logits):
    dp, ctx = lax.axis_index("dp"), lax.axis_index("ctx")
    z, x, y, core = dp // N, dp % N, ctx // 2, ctx % 2
    where = jnp.stack([z, x, y, core]).astype(jnp.int32)
    query = grad_query.reshape(N, 2, QR, N * N * QC)
    key = grad_key.reshape(N, 2, KR, N * N * KC)

    def after(value):
        return lax.optimization_barrier((where, value))[0]

    others, token = [], where
    for step in range(1, N):
        (blocks,) = local(None, step, token, query, key, max_logits)
        token = after(blocks)
        others.append(swap(blocks))
    pre = [local(1, None, where, query, key, max_logits, others[0])]
    *sums, blocks = local(2, N, after(pre[0][0]), query, key, max_logits, others[1])
    pre.append(sums)
    others.append(swap(blocks))
    for step in range(3, N + 1):
        pre.append(local(step, None, where, query, key, max_logits, others[step - 1]))

    p, m, c = pre[0]
    for step in range(1, N):
        p = shift(p, ("x", "z"), (1, 1))
        m = shift(m, ("x", "z"), (-1, -1))
        c = shift(c, ("y", "y"), (1, -1))
        if step < N - 1:
            p, m, c = add(pre[step][0], p), add(pre[step][1], m), add_c(pre[step][2], c)
        if step == 1:
            theirs = swap(lax.dynamic_slice_in_dim(query_moment, (1 - after(c)[3]) * RP, RP, 0))
    pre = pre[-1]

    part = split_ab(where, pre[:2], (p, m))
    part_c = split_c(after(part[0]), pre[2], c)
    part, part_c = scatter(part, ("y", "x")), scatter(part_c, ("z", "z"))
    part = next_parts(next_ab_kernel, "next_ab", where, part)
    part_c = next_parts(next_c_kernel, "next_c", after(part[0]), part_c)
    part, part_c = scatter(part, ("z", "y")), scatter(part_c, ("x", "x"))
    moment, new_key_moment, gram0, gram1, peak = moments(
        where, part, part_c, query_moment, theirs, key_moment
    )

    keep, give = jnp.where(core == 0, gram0, gram1), jnp.where(core == 0, gram1, gram0)
    gram = keep + swap(give)
    own = chain([gram] + [shift(gram, ("y", "y"), (by, by)) for by in (1, 2, 3)])

    theirs = swap(lax.dynamic_slice_in_dim(moment, (1 - core) * RP, RP, 0))
    new_query_moment = jnp.concatenate(
        [
            jnp.where(core == 0, moment[:RP], theirs),
            jnp.where(core == 0, theirs, moment[RP : 2 * RP]),
            moment[2 * RP :],
        ]
    )
    block = update(
        where, own, swap(own), peak, new_query_moment, new_key_moment, query_weight, key_weight
    )
    blocks = [block] + [shift(block, ("z", "x"), (by, by)) for by in (1, 2, 3)]

    def along(stack, by):
        return shift(stack, ("x", "z"), (by, by))

    first, second = (jnp.stack([b[i * M_HALF : (i + 1) * M_HALF] for b in blocks]) for i in range(2))
    first_back, second_ahead = along(first, 1), along(second, -1)
    second_back, first_ahead = along(second, 1), along(first, -1)
    first_far, second_far = along(first_back, 1), along(second_ahead, -1)
    query_out, key_out = assemble(
        where,
        (first, first_back, first_far, first_ahead),
        (second, second_back, second_far, second_ahead),
    )
    return (query_out, key_out, new_query_moment, new_key_moment)


def solution(mesh):
    in_specs = (
        P(("dp", "ctx"), None, None),
        P(("dp", "ctx"), None, None),
        P("ctx", "dp"),
        P("ctx", "dp"),
        P("ctx", "dp"),
        P("ctx", "dp"),
        P(("dp", "ctx"), None),
    )
    out_specs = (P("ctx", None), P("ctx", None), P("ctx", "dp"), P("ctx", "dp"))
    return jax.shard_map(
        on_device, mesh=mesh, in_specs=in_specs, out_specs=out_specs, check_vma=False
    )
```

```python
import functools
import math

import jax
import jax.numpy as jnp
from jax import lax
from jax.experimental import pallas as pl
from jax.experimental.pallas import tpu as pltpu
from jax.sharding import PartitionSpec as P

QL = 1536
KVL = 512
QH = 192
QROPE = 64
KH = 128
ITERS = 5

momentum_decay = 0.9
learn_rate = 0.2
weight_decay = 0.1
clip_limit = 100.0
norm_epsilon = 1e-07
coef_first = 3.4445
coef_second = -4.775
coef_third = 2.0315

N = 4
QC, KC = 384, 256
QR, KR = 192, 64
RP, RC = 80, 32
MP = RP * 3
MC = RC * 3 + KR * 2
ML = 16
M_ALL = 2 * MP + MC
G_ROWS = 288

f32, bf16 = jnp.float32, jnp.bfloat16
AXES = ("dp", "ctx")
VMEM = pl.BlockSpec(memory_space=pltpu.VMEM)
SMEM = pl.BlockSpec(memory_space=pltpu.SMEM)
HBM = pl.BlockSpec(memory_space=pltpu.HBM)
HIGHEST = lax.Precision.HIGHEST


def params(mib):
    return pltpu.CompilerParams(vmem_limit_bytes=mib << 20)


def out(shape, dtype):
    return jax.ShapeDtypeStruct(shape, dtype)


def place(z, x, y, c):
    return ((z % N) * N + x % N) * 2 * N + (y % N) * 2 + c


def shift(array, axes, steps):
    def target(z, x, y, c):
        axis, by = axes[c], steps[c]
        return (z + by * (axis == "z"), x + by * (axis == "x"), y + by * (axis == "y"), c)

    pairs = [
        (place(z, x, y, c), place(*target(z, x, y, c)))
        for z in range(N)
        for x in range(N)
        for y in range(N)
        for c in range(2)
    ]
    return lax.ppermute(array, AXES, pairs)


def swap(array):
    pairs = [(i, i ^ 1) for i in range(2 * N**3)]
    return lax.ppermute(array, AXES, pairs)


def read(where):
    return where[0], where[1], where[2], where[3]


def columns(zz, xx, width, lane=None):
    start = (zz * N + xx) * width
    if lane is None:
        return pl.ds(pl.multiple_of(start, 128), width)
    return pl.ds(pl.multiple_of(start + lane * 128, 128), 128)


def slice_copies(where, other, step, query, key, logits, scratch):
    blocks, c_query, c_key, own_logits, sems = scratch
    z, x, y, core = read(where)
    if other:
        core = 1 - core
    ahead = N - step
    here = jnp.where(core == 0, x, z) + N
    block_c = (y + (1 - 2 * core) * ahead + N) % N
    main = []
    for i in range(N):
        for owner, block in ((0, (here + ahead) % N), (1, (here - ahead) % N)):
            start = jnp.where(core == 0, i * N + block, block * N + i) * QC
            main.append(
                pltpu.make_async_copy(
                    query.at[
                        :,
                        owner,
                        pl.ds(pl.multiple_of(core * RP, 16), RP),
                        pl.ds(pl.multiple_of(start, 128), QC),
                    ],
                    blocks.at[owner, i],
                    sems.at[owner * N + i],
                )
            )
    rest = [pltpu.make_async_copy(logits, own_logits, sems.at[2 * N])]
    for half in range(2):
        rows = pl.ds(half * RC // 2, RC // 2)
        rest.append(
            pltpu.make_async_copy(
                query.at[block_c, core, pl.ds(2 * RP + half * RC // 2, RC // 2), :],
                c_query.at[rows, :],
                sems.at[2 * N + 1 + 2 * half],
            )
        )
        rows = pl.ds(half * KR // 2, KR // 2)
        rest.append(
            pltpu.make_async_copy(
                key.at[block_c, core, rows, :],
                c_key.at[rows, :],
                sems.at[2 * N + 2 + 2 * half],
            )
        )
    return core, main, rest


def split_logits(value):
    high = value.astype(bf16)
    rest = value - high.astype(f32)
    middle = rest.astype(bf16)
    low = (rest - middle.astype(f32)).astype(bf16)
    return high, middle, low


def join_logits(rows):
    rows = rows.astype(f32)
    return rows[0:1] + rows[1:2] + rows[2:3]


def logit_rows(value):
    high, middle, low = (part.astype(f32) for part in split_logits(value))
    row = lax.broadcasted_iota(jnp.int32, (ML, 128), 0)
    return jnp.where(row == 0, high, jnp.where(row == 1, middle, jnp.where(row == 2, low, 0.0)))


def slice_scratch():
    return [
        pltpu.VMEM((2, N, N, RP, QC), bf16),
        pltpu.VMEM((RC, N * N * QC), bf16),
        pltpu.VMEM((KR, N * N * KC), bf16),
        pltpu.VMEM((1, 32), f32),
        pltpu.SemaphoreType.DMA((2 * N + 5,)),
    ]


N_SCRATCH = 5


def in_hbm(*arrays):
    return tuple(pltpu.with_memory_space_constraint(a, pltpu.HBM) for a in arrays)


def in_hbm(*arrays):
    return tuple(pltpu.with_memory_space_constraint(a, pltpu.HBM) for a in arrays)


def total(*terms):
    value = terms[0].astype(f32)
    for term in terms[1:]:
        value = value + term.astype(f32)
    return value


def most(*terms):
    value = join_logits(terms[0])
    for term in terms[1:]:
        value = jnp.maximum(value, join_logits(term))
    return logit_rows(value)


C_PIECES = ((0, RC, 3, 0, QC), (1, KR, 2, 3 * RC, KC))


def sum_blocks(work, other, lanes, p, m, c):
    (core, main, rest), (blocks, c_query, c_key, own_logits, _) = work
    for copy in rest:
        copy.wait()
    lanes[pl.ds(0, 1), pl.ds(0, 32)] = own_logits[...]
    peak = jnp.maximum(lanes[pl.ds(0, 1), :], join_logits(other[0, 0, pl.ds(M_ALL, ML), :]))
    logit_block = logit_rows(peak).astype(bf16)

    @pl.loop(0, N * N)
    def _(i):
        at = (i // N, i % N)
        c[at + (pl.ds(MC, ML),)] = logit_block
        for source, height, width, start, size in C_PIECES:
            for lane in range(width):
                rows = start + lane * height
                c[at + (pl.ds(rows, height),)] = total(
                    (c_query, c_key)[source][:, columns(at[0], at[1], size, lane)],
                    other[at + (pl.ds(2 * MP + rows, height),)],
                ).astype(bf16)

    for i in range(N):
        main[2 * i].wait()
        main[2 * i + 1].wait()

        @pl.loop(0, N)
        def _(j):
            first, second = jnp.where(core == 0, j, i), jnp.where(core == 0, i, j)
            for owner, to in ((0, p), (1, m)):
                block = blocks[owner, i, j]
                for lane in range(3):
                    to[first, second, pl.ds(lane * RP, RP), :] = total(
                        block[:, lane * 128 : (lane + 1) * 128],
                        other[first, second, pl.ds(owner * MP + lane * RP, RP), :],
                    ).astype(bf16)


def collect_blocks(work, lanes, to):
    (core, main, rest), (blocks, c_query, c_key, own_logits, _) = work
    for copy in rest:
        copy.wait()
    lanes[pl.ds(0, 1), pl.ds(0, 32)] = own_logits[...]
    logit_block = logit_rows(lanes[pl.ds(0, 1), :]).astype(bf16)

    @pl.loop(0, N * N)
    def _(i):
        at = (i // N, i % N)
        to[at + (pl.ds(M_ALL, ML),)] = logit_block
        for source, height, width, start, size in C_PIECES:
            for lane in range(width):
                to[at + (pl.ds(2 * MP + start + lane * height, height),)] = (c_query, c_key)[
                    source
                ][:, columns(at[0], at[1], size, lane)]

    for i in range(N):
        main[2 * i].wait()
        main[2 * i + 1].wait()

        @pl.loop(0, N)
        def _(j):
            first, second = jnp.where(core == 0, j, i), jnp.where(core == 0, i, j)
            for owner in range(2):
                block = blocks[owner, i, j]
                for lane in range(3):
                    to[first, second, pl.ds(owner * MP + lane * RP, RP), :] = block[
                        :, lane * 128 : (lane + 1) * 128
                    ]


def local_kernel(sum_step, send_step, where, query, key, logits, *refs):
    refs = list(refs)
    other = [refs.pop(0)] if sum_step else []
    sums = [refs.pop(0) for _ in range(3)] if sum_step else []
    to = [refs.pop(0)] if send_step else []
    lanes = refs.pop()
    works = []
    for step, is_other in ((sum_step, False), (send_step, True)):
        if step:
            scratch, refs = refs[:N_SCRATCH], refs[N_SCRATCH:]
            copies = slice_copies(where, is_other, step, query, key, logits, scratch)
            for copy in copies[2] + copies[1]:
                copy.start()
            works.append((copies, scratch))
    lanes[...] = jnp.zeros_like(lanes)
    if sum_step:
        sum_blocks(works[0], *other, lanes, *sums)
    if send_step:
        collect_blocks(works[-1], lanes, *to)


def local(sum_step, send_step, where, query, key, logits, other=None):
    shapes, scratch, inputs = [], [], list(in_hbm(query, key, logits))
    if sum_step:
        shapes += [out((N, N, height, 128), bf16) for height in (MP, MP, MC + ML)]
        scratch += slice_scratch()
        inputs.append(other)
    if send_step:
        shapes += [out((N, N, M_ALL + ML, 128), bf16)]
        scratch += slice_scratch()
    return pl.pallas_call(
        functools.partial(local_kernel, sum_step, send_step),
        out_shape=shapes,
        in_specs=[SMEM, HBM, HBM, HBM] + [VMEM] * (1 if sum_step else 0),
        out_specs=[VMEM] * len(shapes),
        scratch_shapes=scratch + [pltpu.VMEM((8, 128), f32)],
        compiler_params=params(15 if sum_step and send_step else 10 if sum_step else 7),
        name=f"local_sum_{sum_step}_send_{send_step}",
    )(where, *inputs)


def add(first, second):
    return (first.astype(f32) + second.astype(f32)).astype(bf16)


def add_c_kernel(first, second, to):
    peak = most(first[0, 0, pl.ds(MC, ML), :], second[0, 0, pl.ds(MC, ML), :]).astype(bf16)

    @pl.loop(0, N * N)
    def _(i):
        rows = (i // N, i % N, pl.ds(0, MC))
        to[rows] = total(first[rows], second[rows]).astype(bf16)
        to[i // N, i % N, pl.ds(MC, ML), :] = peak


def add_c(first, second):
    return pl.pallas_call(
        add_c_kernel,
        out_shape=out((N, N, MC + ML, 128), bf16),
        in_specs=[VMEM, VMEM],
        out_specs=VMEM,
        compiler_params=params(6),
        name="add_c",
    )(first, second)


def split_ab_kernel(where, p0, m0, p1, m1, *outs):
    _, x, y, core = read(where)
    here = jnp.where(core == 0, y, x)
    for by, to in enumerate(outs):
        block = (here + by) % N

        @pl.loop(0, N)
        def _(i):
            to[i, pl.ds(0, MP), :] = total(p0[block, i], p1[block, i]).astype(bf16)
            to[i, pl.ds(MP, MP), :] = total(m0[block, i], m1[block, i]).astype(bf16)


def split_ab(where, own, received):
    return pl.pallas_call(
        split_ab_kernel,
        out_shape=[out((N, 2 * MP, 128), bf16)] * N,
        in_specs=[SMEM] + [VMEM] * 4,
        out_specs=[VMEM] * N,
        compiler_params=params(10),
        name="split_ab",
    )(where, *own, *received)


def split_c_kernel(where, c0, c1, *outs):
    peak = most(c0[0, 0, pl.ds(MC, ML), :], c1[0, 0, pl.ds(MC, ML), :]).astype(bf16)
    for by, to in enumerate(outs):
        block = (where[0] + by) % N

        @pl.loop(0, N)
        def _(i):
            rows = (block, i, pl.ds(0, MC))
            to[i, pl.ds(0, MC), :] = total(c0[rows], c1[rows]).astype(bf16)
            to[i, pl.ds(MC, ML), :] = peak


def split_c(where, own, received):
    return pl.pallas_call(
        split_c_kernel,
        out_shape=[out((N, MC + ML, 128), bf16)] * N,
        in_specs=[SMEM] + [VMEM] * 2,
        out_specs=[VMEM] * N,
        compiler_params=params(6),
        name="split_c",
    )(where, own, received)


def next_ab_kernel(where, t0, t1, t2, t3, *outs):
    z, _, y, core = read(where)
    here = jnp.where(core == 0, z, y)
    for by, to in enumerate(outs):
        block = (here + by) % N
        to[...] = total(t0[block], t1[block], t2[block], t3[block]).astype(bf16)


def next_c_kernel(where, t0, t1, t2, t3, *outs):
    terms = (t0, t1, t2, t3)
    peak = most(*(t[0, pl.ds(MC, ML), :] for t in terms)).astype(bf16)
    for by, to in enumerate(outs):
        rows = ((where[1] + by) % N, pl.ds(0, MC))
        to[pl.ds(0, MC), :] = total(*(t[rows] for t in terms)).astype(bf16)
        to[pl.ds(MC, ML), :] = peak


def next_parts(kernel, name, where, terms):
    return pl.pallas_call(
        kernel,
        out_shape=[out((terms[0].shape[1], 128), bf16)] * N,
        in_specs=[SMEM] + [VMEM] * N,
        out_specs=[VMEM] * N,
        compiler_params=params(6),
        name=name,
    )(where, *terms)


def scatter(blocks, axes):
    return [blocks[0]] + [shift(blocks[by], axes, (by, by)) for by in (1, 2, 3)]


def moment_kernel(
    where, a0, a1, a2, a3, c0, c1, c2, c3, qm, theirs, km, qm_out, km_out, gram0, gram1, peak
):
    core = where[3]
    part = total(a0[...], a1[...], a2[...], a3[...])
    rows = pl.ds(0, MC)
    part_c = total(c0[rows, :], c1[rows, :], c2[rows, :], c3[rows, :])
    rows = pl.ds(MC, ML)
    value = join_logits(c0[rows, :])
    for ref in (c1, c2, c3):
        value = jnp.maximum(value, join_logits(ref[rows, :]))
    peak[...] = jnp.broadcast_to(value, (8, 128))
    for lane in range(3):
        lanes = pl.ds(lane * 128, 128)
        for owner in range(2):
            rows = pl.ds(owner * RP, RP)
            start = owner * MP + lane * RP
            moment = jnp.where(core == owner, qm[rows, lanes], theirs[:, lanes])
            qm_out[rows, lanes] = momentum_decay * moment + part[start : start + RP]
        rows = pl.ds(2 * RP, RC)
        qm_out[rows, lanes] = (
            momentum_decay * qm[rows, lanes] + part_c[lane * RC : (lane + 1) * RC]
        )
    for lane in range(2):
        lanes = pl.ds(lane * 128, 128)
        start = 3 * RC + lane * KR
        km_out[:, lanes] = momentum_decay * km[:, lanes] + part_c[start : start + KR]

    def gram_of(value):
        return lax.dot_general(
            value, value, (((0,), (0,)), ((), ())), precision=HIGHEST, preferred_element_type=f32
        )

    full = qm_out[...]
    for head, to in enumerate((gram0, gram1)):
        wide = (full if head == 0 else pltpu.roll(full, QH, 1))[:, :256]
        gram = gram_of(wide)
        left = lax.broadcasted_iota(jnp.int32, (64, 128), 1) < 64
        to[pl.ds(0, 64), :] = jnp.where(
            left, gram[:64, :128], pltpu.roll(gram[128:192, 128:], 64, 1)
        )
        to[pl.ds(64, 128), :] = gram[64:192, :128]
        gram = gram_of(km_out[:, pl.ds(head * KH, KH)])
        to[pl.ds(192, 64), :] = gram[64:]
        to[pl.ds(256, 32), :] = jnp.where(left[:32], gram[:32], pltpu.roll(gram[32:64], 64, 1))


def moments(where, part, part_c, query_moment, theirs, key_moment):
    return pl.pallas_call(
        moment_kernel,
        out_shape=(
            out((QR, QC), f32),
            out((KR, KC), f32),
            out((G_ROWS, 128), f32),
            out((G_ROWS, 128), f32),
            out((8, 128), f32),
        ),
        in_specs=[SMEM] + [VMEM] * 11,
        out_specs=(VMEM,) * 5,
        compiler_params=params(12),
        name="moments",
    )(where, *part, *part_c, query_moment, theirs, key_moment)


def three_products(left, right):
    def halves(value):
        high = value.astype(bf16)
        return high, (value - high.astype(f32)).astype(bf16)

    def product(first, second):
        return jnp.dot(first, second, preferred_element_type=f32)

    (left_high, left_low), (right_high, right_low) = halves(left), halves(right)
    return product(left_high, right_high) + (
        product(left_high, right_low) + product(left_low, right_high)
    )


def chain_kernel(g0, g1, g2, g3, to):
    packed = g0[...] + g1[...] + g2[...] + g3[...]
    row = lax.broadcasted_iota(jnp.int32, (256, 256), 0)
    column = lax.broadcasted_iota(jnp.int32, (256, 256), 1)
    left = lax.broadcasted_iota(jnp.int32, (64, 128), 1) < 64
    zeros = jnp.zeros((64, 128), f32)

    def stacked(*blocks):
        return jnp.concatenate(blocks, axis=0)

    def part(block, keep_left):
        return jnp.where(left if keep_left else ~left, block, 0.0)

    diagonal, middle, last = packed[:64], packed[64:128], packed[128:192]
    lower = stacked(zeros, part(middle, True), last, zeros)
    first = lower + stacked(part(diagonal, True), part(middle, False), zeros, zeros)
    corner = part(pltpu.roll(diagonal, 64, 1), True)
    query_gram = jnp.concatenate(
        [first, stacked(zeros, zeros, corner, zeros)], axis=1
    ) + stacked(lower.T, jnp.zeros((128, 256), f32))
    middle, diagonal = packed[192:256], packed[256:288]
    lower = stacked(zeros, part(middle, True))
    diagonal = part(stacked(diagonal, pltpu.roll(diagonal, 64, 1)), True)
    key_gram = lower + lower.T + stacked(diagonal, part(middle, False))
    query_eye = jnp.where((row == column) & (row < QH), 1.0, 0.0).astype(f32)
    key_eye = jnp.where(row == column, 1.0, 0.0).astype(f32)[:128, :128]

    def product(left, right, exact):
        if exact:
            return jnp.dot(left, right, precision=HIGHEST, preferred_element_type=f32)
        return three_products(left, right)

    def start(gram, eye):
        square = jnp.sum(jnp.sum(gram * eye, axis=1, keepdims=True), axis=0, keepdims=True)
        inverse = 1.0 / (jnp.sqrt(square) + norm_epsilon)
        return gram * inverse * inverse, inverse

    grams, inverses = zip(start(query_gram, query_eye), start(key_gram, key_eye))
    grams, eyes, totals = list(grams), (query_eye, key_eye), [None, None]
    for iteration in range(ITERS):
        exact = iteration < 2
        mixers = []
        for i in range(2):
            square = product(grams[i], grams[i], exact)
            mixers.append(coef_first * eyes[i] + coef_second * grams[i] + coef_third * square)
        if iteration < ITERS - 1:
            halves = [product(mixers[i], grams[i], exact) for i in range(2)]
        for i in range(2):
            totals[i] = mixers[i] if iteration == 0 else product(totals[i], mixers[i], exact)
        if iteration < ITERS - 1:
            grams = [product(halves[i], mixers[i], exact) for i in range(2)]
    query_total, key_total = (totals[i] * inverses[i] for i in range(2))
    to[pl.ds(0, 192), :] = query_total[:192, :128]
    to[pl.ds(192, 192), :] = query_total[:192, 128:]
    to[pl.ds(384, 128), :] = key_total


def chain(grams):
    return pl.pallas_call(
        chain_kernel,
        out_shape=out((512, 128), f32),
        in_specs=[VMEM] * 4,
        out_specs=VMEM,
        compiler_params=params(12),
        name="newton_schulz_polynomial",
    )(*grams)

def update_kernel(where, own, other, peak, qm, km, qw, kw, to):
    z, x, _, core = read(where)
    mine, theirs = own[...], other[...]
    packs = (jnp.where(core == 0, mine, theirs), jnp.where(core == 0, theirs, mine))

    product = three_products
    gamma = jnp.minimum(1.0, clip_limit / peak[pl.ds(0, 1), :])
    lane = lax.broadcasted_iota(jnp.int32, (1, 128), 1)
    first_head = 2 * (z * N + x)
    gammas = [
        jnp.sum(jnp.where(lane == first_head + h, gamma, 0.0), axis=1, keepdims=True)
        for h in range(2)
    ]
    roots = [jnp.sqrt(g) for g in gammas]
    column = lax.broadcasted_iota(jnp.int32, (1, QC), 1)
    second = column >= QH
    rope = jnp.where(second, column - QH, column) >= QH - QROPE
    query_factor = jnp.where(
        rope, jnp.where(second, gammas[1], gammas[0]), jnp.where(second, roots[1], roots[0])
    )
    key_factor = jnp.where(
        lax.broadcasted_iota(jnp.int32, (1, KC), 1) >= KH, roots[1], roots[0]
    )

    full = qm[...]
    zeros = jnp.zeros((64, 256), f32)
    pad = jnp.zeros((QR, 128), f32)
    pieces = []
    for head in range(2):
        wide = (full if head == 0 else pltpu.roll(full, QH, 1))[:, :256]
        matrix = jnp.concatenate([packs[head][:192], packs[head][192:384]], axis=1)
        matrix = jnp.concatenate([matrix, zeros], axis=0)
        piece = jnp.concatenate([product(wide, matrix), pad], axis=1)
        pieces.append(piece if head == 0 else pltpu.roll(piece, QH, 1))
    query_ortho = pieces[0] + pieces[1]
    key_ortho = jnp.concatenate(
        [product(km[:, pl.ds(h * KH, KH)], packs[h][384:]) for h in range(2)], axis=1
    )
    query_scale = 0.2 * math.sqrt(max(QL, QH))
    key_scale = 0.2 * math.sqrt(max(KVL, KH))
    query_weight, key_weight = qw[...], kw[...]
    query_next = query_weight - learn_rate * (
        query_scale * query_ortho + weight_decay * query_weight
    )
    key_next = key_weight - learn_rate * (key_scale * key_ortho + weight_decay * key_weight)
    query_block = (query_next * query_factor).astype(bf16)
    key_block = (key_next * key_factor).astype(bf16)
    for lane in range(3):
        to[pl.ds(lane * QR, QR), :] = query_block[:, lane * 128 : (lane + 1) * 128]
    for lane in range(2):
        to[pl.ds(3 * QR + lane * KR, KR), :] = key_block[:, lane * 128 : (lane + 1) * 128]


def update(where, own, other, peak, query_moment, key_moment, query_weight, key_weight):
    return pl.pallas_call(
        update_kernel,
        out_shape=out((M_ALL, 128), bf16),
        in_specs=[SMEM] + [VMEM] * 7,
        out_specs=VMEM,
        compiler_params=params(12),
        name="update",
    )(where, own, other, peak, query_moment, key_moment, query_weight, key_weight)


def gathered_pieces(where, far, i, stack, query_out, key_out):
    z, x, _, core = read(where)
    for j in range(2):
        near = 2 * i + j
        back_z, back_x = jnp.where(core == 0, near, far), jnp.where(core == 0, far, near)
        zz, xx = (z + N - back_z) % N, (x + N - back_x) % N
        for lane in range(3):
            rows = pl.ds(lane * QR, QR)
            yield stack.at[j, rows, :], query_out.at[:, columns(zz, xx, QC, lane)]
        for lane in range(2):
            rows = pl.ds(3 * QR + lane * KR, KR)
            yield stack.at[j, rows, :], key_out.at[:, columns(zz, xx, KC, lane)]


def assemble_kernel(where, f0, f1, f3, s0, s1, s3, query_out, key_out):
    for i, stacks in enumerate(((f0, f1, f3), (s0, s1, s3))):
        for far, stack in zip((0, 1, 3), stacks):
            for source, to in gathered_pieces(where, far, i, stack, query_out, key_out):
                to[...] = source[...]


RESULT = (pltpu.HBM((QR, N * N * QC), bf16), pltpu.HBM((KR, N * N * KC), bf16))


def assemble(where, first, second):
    return pl.pallas_call(
        assemble_kernel,
        out_shape=RESULT,
        in_specs=[SMEM] + [VMEM] * 6,
        out_specs=(VMEM, VMEM),
        compiler_params=params(16),
        name="assemble",
    )(where, *first, *second)


def finish_kernel(where, query_in, key_in, first, second, query_out, key_out, sems):
    copies = []
    for i, stack in enumerate((first, second)):
        for source, to in gathered_pieces(where, 2, i, stack, query_out, key_out):
            copies.append(pltpu.make_async_copy(source, to, sems.at[len(copies)]))
    for copy in copies:
        copy.start()
    for copy in copies:
        copy.wait()


def finish(where, query_out, key_out, first, second):
    return pl.pallas_call(
        finish_kernel,
        out_shape=RESULT,
        in_specs=[SMEM, HBM, HBM, VMEM, VMEM],
        out_specs=(HBM, HBM),
        scratch_shapes=[pltpu.SemaphoreType.DMA((20,))],
        input_output_aliases={1: 0, 2: 1},
        compiler_params=params(4),
        name="finish",
    )(where, *in_hbm(query_out, key_out), first, second)


def on_device(grad_query, grad_key, query_weight, key_weight, query_moment, key_moment, max_logits):
    dp, ctx = lax.axis_index("dp"), lax.axis_index("ctx")
    z, x, y, core = dp // N, dp % N, ctx // 2, ctx % 2
    where = jnp.stack([z, x, y, core]).astype(jnp.int32)
    query = grad_query.reshape(N, 2, QR, N * N * QC)
    key = grad_key.reshape(N, 2, KR, N * N * KC)

    def after(value):
        return lax.optimization_barrier((where, value))[0]

    others, token = [], where
    for step in range(1, N):
        (blocks,) = local(None, step, token, query, key, max_logits)
        token = after(blocks)
        others.append(swap(blocks))
    pre = [local(1, None, where, query, key, max_logits, others[0])]
    *sums, blocks = local(2, N, after(pre[0][0]), query, key, max_logits, others[1])
    pre.append(sums)
    others.append(swap(blocks))
    for step in range(3, N + 1):
        pre.append(local(step, None, where, query, key, max_logits, others[step - 1]))

    p, m, c = pre[0]
    for step in range(1, N):
        p = shift(p, ("x", "z"), (1, 1))
        m = shift(m, ("x", "z"), (-1, -1))
        c = shift(c, ("y", "y"), (1, -1))
        if step < N - 1:
            p, m, c = add(pre[step][0], p), add(pre[step][1], m), add_c(pre[step][2], c)
        if step == 1:
            theirs = swap(lax.dynamic_slice_in_dim(query_moment, (1 - after(c)[3]) * RP, RP, 0))
    pre = pre[-1]

    part = split_ab(where, pre[:2], (p, m))
    part_c = split_c(after(part[0]), pre[2], c)
    part, part_c = scatter(part, ("y", "x")), scatter(part_c, ("z", "z"))
    part = next_parts(next_ab_kernel, "next_ab", where, part)
    part_c = next_parts(next_c_kernel, "next_c", after(part[0]), part_c)
    part, part_c = scatter(part, ("z", "y")), scatter(part_c, ("x", "x"))
    moment, new_key_moment, gram0, gram1, peak = moments(
        where, part, part_c, query_moment, theirs, key_moment
    )

    keep, give = jnp.where(core == 0, gram0, gram1), jnp.where(core == 0, gram1, gram0)
    gram = keep + swap(give)
    own = chain([gram] + [shift(gram, ("y", "y"), (by, by)) for by in (1, 2, 3)])

    theirs = swap(lax.dynamic_slice_in_dim(moment, (1 - core) * RP, RP, 0))
    new_query_moment = jnp.concatenate(
        [
            jnp.where(core == 0, moment[:RP], theirs),
            jnp.where(core == 0, theirs, moment[RP : 2 * RP]),
            moment[2 * RP :],
        ]
    )
    block = update(
        where, own, swap(own), peak, new_query_moment, new_key_moment, query_weight, key_weight
    )
    blocks = [block] + [shift(block, ("z", "x"), (by, by)) for by in (1, 2, 3)]

    def along(stack, by):
        return shift(stack, ("x", "z"), (by, by))

    first, second = jnp.stack(blocks[:2]), jnp.stack(blocks[2:])
    first_back, second_ahead = along(first, 1), along(second, -1)
    second_back, first_ahead = along(second, 1), along(first, -1)
    first_far, second_far = along(first_back, 1), along(second_ahead, -1)
    query_out, key_out = assemble(
        where, (first, first_back, first_ahead), (second, second_back, second_ahead)
    )
    query_out, key_out = finish(where, query_out, key_out, first_far, second_far)
    return (query_out, key_out, new_query_moment, new_key_moment)


def solution(mesh):
    in_specs = (
        P(("dp", "ctx"), None, None),
        P(("dp", "ctx"), None, None),
        P("ctx", "dp"),
        P("ctx", "dp"),
        P("ctx", "dp"),
        P("ctx", "dp"),
        P(("dp", "ctx"), None),
    )
    out_specs = (P("ctx", None), P("ctx", None), P("ctx", "dp"), P("ctx", "dp"))
    return jax.shard_map(
        on_device, mesh=mesh, in_specs=in_specs, out_specs=out_specs, check_vma=False
    )
```

```python
import functools
import math

import jax
import jax.numpy as jnp
from jax import lax
from jax.experimental import pallas as pl
from jax.experimental.pallas import tpu as pltpu
from jax.sharding import PartitionSpec as P

QL = 1536
KVL = 512
QH = 192
QROPE = 64
KH = 128
ITERS = 5

momentum_decay = 0.9
learn_rate = 0.2
weight_decay = 0.1
clip_limit = 100.0
norm_epsilon = 1e-07
coef_first = 3.4445
coef_second = -4.775
coef_third = 2.0315

N = 4
QC, KC = 384, 256
QR, KR = 192, 64
RP, RC = 80, 32
MP = RP * 3
MC = RC * 3 + KR * 2
ML = 16
M_ALL = 2 * MP + MC
G_ROWS = 288

f32, bf16 = jnp.float32, jnp.bfloat16
AXES = ("dp", "ctx")
VMEM = pl.BlockSpec(memory_space=pltpu.VMEM)
SMEM = pl.BlockSpec(memory_space=pltpu.SMEM)
HBM = pl.BlockSpec(memory_space=pltpu.HBM)
HIGHEST = lax.Precision.HIGHEST


def params(mib):
    return pltpu.CompilerParams(vmem_limit_bytes=mib << 20)


def out(shape, dtype):
    return jax.ShapeDtypeStruct(shape, dtype)


def place(z, x, y, c):
    return ((z % N) * N + x % N) * 2 * N + (y % N) * 2 + c


def shift(array, axes, steps):
    def target(z, x, y, c):
        axis, by = axes[c], steps[c]
        return (z + by * (axis == "z"), x + by * (axis == "x"), y + by * (axis == "y"), c)

    pairs = [
        (place(z, x, y, c), place(*target(z, x, y, c)))
        for z in range(N)
        for x in range(N)
        for y in range(N)
        for c in range(2)
    ]
    return lax.ppermute(array, AXES, pairs)


def swap(array):
    pairs = [(i, i ^ 1) for i in range(2 * N**3)]
    return lax.ppermute(array, AXES, pairs)


def read(where):
    return where[0], where[1], where[2], where[3]


def columns(zz, xx, width, lane=None):
    start = (zz * N + xx) * width
    if lane is None:
        return pl.ds(pl.multiple_of(start, 128), width)
    return pl.ds(pl.multiple_of(start + lane * 128, 128), 128)


def slice_copies(where, other, step, query, key, logits, scratch):
    blocks, c_query, c_key, own_logits, sems = scratch
    z, x, y, core = read(where)
    if other:
        core = 1 - core
    ahead = N - step
    here = jnp.where(core == 0, x, z) + N
    block_c = (y + (1 - 2 * core) * ahead + N) % N
    main = []
    for i in range(N):
        for owner, block in ((0, (here + ahead) % N), (1, (here - ahead) % N)):
            start = jnp.where(core == 0, i * N + block, block * N + i) * QC
            main.append(
                pltpu.make_async_copy(
                    query.at[
                        :,
                        owner,
                        pl.ds(pl.multiple_of(core * RP, 16), RP),
                        pl.ds(pl.multiple_of(start, 128), QC),
                    ],
                    blocks.at[owner, i],
                    sems.at[owner * N + i],
                )
            )
    rest = [pltpu.make_async_copy(logits, own_logits, sems.at[2 * N])]
    for half in range(2):
        rows = pl.ds(half * RC // 2, RC // 2)
        rest.append(
            pltpu.make_async_copy(
                query.at[block_c, core, pl.ds(2 * RP + half * RC // 2, RC // 2), :],
                c_query.at[rows, :],
                sems.at[2 * N + 1 + 2 * half],
            )
        )
        rows = pl.ds(half * KR // 2, KR // 2)
        rest.append(
            pltpu.make_async_copy(
                key.at[block_c, core, rows, :],
                c_key.at[rows, :],
                sems.at[2 * N + 2 + 2 * half],
            )
        )
    return core, main, rest


def split_logits(value):
    high = value.astype(bf16)
    rest = value - high.astype(f32)
    middle = rest.astype(bf16)
    low = (rest - middle.astype(f32)).astype(bf16)
    return high, middle, low


def join_logits(rows):
    rows = rows.astype(f32)
    return rows[0:1] + rows[1:2] + rows[2:3]


def logit_rows(value):
    high, middle, low = (part.astype(f32) for part in split_logits(value))
    row = lax.broadcasted_iota(jnp.int32, (ML, 128), 0)
    return jnp.where(row == 0, high, jnp.where(row == 1, middle, jnp.where(row == 2, low, 0.0)))


def slice_scratch():
    return [
        pltpu.VMEM((2, N, N, RP, QC), bf16),
        pltpu.VMEM((RC, N * N * QC), bf16),
        pltpu.VMEM((KR, N * N * KC), bf16),
        pltpu.VMEM((1, 32), f32),
        pltpu.SemaphoreType.DMA((2 * N + 5,)),
    ]


N_SCRATCH = 5


def in_hbm(*arrays):
    return tuple(pltpu.with_memory_space_constraint(a, pltpu.HBM) for a in arrays)


def in_hbm(*arrays):
    return tuple(pltpu.with_memory_space_constraint(a, pltpu.HBM) for a in arrays)


def total(*terms):
    value = terms[0].astype(f32)
    for term in terms[1:]:
        value = value + term.astype(f32)
    return value


def most(*terms):
    value = join_logits(terms[0])
    for term in terms[1:]:
        value = jnp.maximum(value, join_logits(term))
    return logit_rows(value)


C_PIECES = ((0, RC, 3, 0, QC), (1, KR, 2, 3 * RC, KC))


def sum_blocks(work, other, lanes, p, m, c):
    (core, main, rest), (blocks, c_query, c_key, own_logits, _) = work
    for copy in rest:
        copy.wait()
    lanes[pl.ds(0, 1), pl.ds(0, 32)] = own_logits[...]
    peak = jnp.maximum(lanes[pl.ds(0, 1), :], join_logits(other[0, 0, pl.ds(M_ALL, ML), :]))
    logit_block = logit_rows(peak).astype(bf16)

    @pl.loop(0, N * N)
    def _(i):
        at = (i // N, i % N)
        c[at + (pl.ds(MC, ML),)] = logit_block
        for source, height, width, start, size in C_PIECES:
            for lane in range(width):
                rows = start + lane * height
                c[at + (pl.ds(rows, height),)] = total(
                    (c_query, c_key)[source][:, columns(at[0], at[1], size, lane)],
                    other[at + (pl.ds(2 * MP + rows, height),)],
                ).astype(bf16)

    for i in range(N):
        main[2 * i].wait()
        main[2 * i + 1].wait()

        @pl.loop(0, N)
        def _(j):
            first, second = jnp.where(core == 0, j, i), jnp.where(core == 0, i, j)
            for owner, to in ((0, p), (1, m)):
                block = blocks[owner, i, j]
                for lane in range(3):
                    to[first, second, pl.ds(lane * RP, RP), :] = total(
                        block[:, lane * 128 : (lane + 1) * 128],
                        other[first, second, pl.ds(owner * MP + lane * RP, RP), :],
                    ).astype(bf16)


def collect_blocks(work, lanes, to):
    (core, main, rest), (blocks, c_query, c_key, own_logits, _) = work
    for copy in rest:
        copy.wait()
    lanes[pl.ds(0, 1), pl.ds(0, 32)] = own_logits[...]
    logit_block = logit_rows(lanes[pl.ds(0, 1), :]).astype(bf16)

    @pl.loop(0, N * N)
    def _(i):
        at = (i // N, i % N)
        to[at + (pl.ds(M_ALL, ML),)] = logit_block
        for source, height, width, start, size in C_PIECES:
            for lane in range(width):
                to[at + (pl.ds(2 * MP + start + lane * height, height),)] = (c_query, c_key)[
                    source
                ][:, columns(at[0], at[1], size, lane)]

    for i in range(N):
        main[2 * i].wait()
        main[2 * i + 1].wait()

        @pl.loop(0, N)
        def _(j):
            first, second = jnp.where(core == 0, j, i), jnp.where(core == 0, i, j)
            for owner in range(2):
                block = blocks[owner, i, j]
                for lane in range(3):
                    to[first, second, pl.ds(owner * MP + lane * RP, RP), :] = block[
                        :, lane * 128 : (lane + 1) * 128
                    ]


def local_kernel(sum_step, send_step, where, query, key, logits, *refs):
    refs = list(refs)
    other = [refs.pop(0)] if sum_step else []
    sums = [refs.pop(0) for _ in range(3)] if sum_step else []
    to = [refs.pop(0)] if send_step else []
    lanes = refs.pop()
    works = []
    for step, is_other in ((sum_step, False), (send_step, True)):
        if step:
            scratch, refs = refs[:N_SCRATCH], refs[N_SCRATCH:]
            copies = slice_copies(where, is_other, step, query, key, logits, scratch)
            for copy in copies[2] + copies[1]:
                copy.start()
            works.append((copies, scratch))
    lanes[...] = jnp.zeros_like(lanes)
    if sum_step:
        sum_blocks(works[0], *other, lanes, *sums)
    if send_step:
        collect_blocks(works[-1], lanes, *to)


def local(sum_step, send_step, where, query, key, logits, other=None):
    shapes, scratch, inputs = [], [], list(in_hbm(query, key, logits))
    if sum_step:
        shapes += [out((N, N, height, 128), bf16) for height in (MP, MP, MC + ML)]
        scratch += slice_scratch()
        inputs.append(other)
    if send_step:
        shapes += [out((N, N, M_ALL + ML, 128), bf16)]
        scratch += slice_scratch()
    return pl.pallas_call(
        functools.partial(local_kernel, sum_step, send_step),
        out_shape=shapes,
        in_specs=[SMEM, HBM, HBM, HBM] + [VMEM] * (1 if sum_step else 0),
        out_specs=[VMEM] * len(shapes),
        scratch_shapes=scratch + [pltpu.VMEM((8, 128), f32)],
        compiler_params=params(15 if sum_step and send_step else 10 if sum_step else 7),
        name=f"local_sum_{sum_step}_send_{send_step}",
    )(where, *inputs)


def add(first, second):
    return (first.astype(f32) + second.astype(f32)).astype(bf16)


def add_c_kernel(first, second, to):
    peak = most(first[0, 0, pl.ds(MC, ML), :], second[0, 0, pl.ds(MC, ML), :]).astype(bf16)

    @pl.loop(0, N * N)
    def _(i):
        rows = (i // N, i % N, pl.ds(0, MC))
        to[rows] = total(first[rows], second[rows]).astype(bf16)
        to[i // N, i % N, pl.ds(MC, ML), :] = peak


def add_c(first, second):
    return pl.pallas_call(
        add_c_kernel,
        out_shape=out((N, N, MC + ML, 128), bf16),
        in_specs=[VMEM, VMEM],
        out_specs=VMEM,
        compiler_params=params(6),
        name="add_c",
    )(first, second)


def split_ab_kernel(where, p0, m0, p1, m1, *outs):
    _, x, y, core = read(where)
    here = jnp.where(core == 0, y, x)
    for by, to in enumerate(outs):
        block = (here + by) % N

        @pl.loop(0, N)
        def _(i):
            to[i, pl.ds(0, MP), :] = total(p0[block, i], p1[block, i]).astype(bf16)
            to[i, pl.ds(MP, MP), :] = total(m0[block, i], m1[block, i]).astype(bf16)


def split_ab(where, own, received):
    return pl.pallas_call(
        split_ab_kernel,
        out_shape=[out((N, 2 * MP, 128), bf16)] * N,
        in_specs=[SMEM] + [VMEM] * 4,
        out_specs=[VMEM] * N,
        compiler_params=params(10),
        name="split_ab",
    )(where, *own, *received)


def split_c_kernel(where, c0, c1, *outs):
    peak = most(c0[0, 0, pl.ds(MC, ML), :], c1[0, 0, pl.ds(MC, ML), :]).astype(bf16)
    for by, to in enumerate(outs):
        block = (where[0] + by) % N

        @pl.loop(0, N)
        def _(i):
            rows = (block, i, pl.ds(0, MC))
            to[i, pl.ds(0, MC), :] = total(c0[rows], c1[rows]).astype(bf16)
            to[i, pl.ds(MC, ML), :] = peak


def split_c(where, own, received):
    return pl.pallas_call(
        split_c_kernel,
        out_shape=[out((N, MC + ML, 128), bf16)] * N,
        in_specs=[SMEM] + [VMEM] * 2,
        out_specs=[VMEM] * N,
        compiler_params=params(6),
        name="split_c",
    )(where, own, received)


def next_ab_kernel(where, t0, t1, t2, t3, *outs):
    z, _, y, core = read(where)
    here = jnp.where(core == 0, z, y)
    for by, to in enumerate(outs):
        block = (here + by) % N
        to[...] = total(t0[block], t1[block], t2[block], t3[block]).astype(bf16)


def next_c_kernel(where, t0, t1, t2, t3, *outs):
    terms = (t0, t1, t2, t3)
    peak = most(*(t[0, pl.ds(MC, ML), :] for t in terms)).astype(bf16)
    for by, to in enumerate(outs):
        rows = ((where[1] + by) % N, pl.ds(0, MC))
        to[pl.ds(0, MC), :] = total(*(t[rows] for t in terms)).astype(bf16)
        to[pl.ds(MC, ML), :] = peak


def next_parts(kernel, name, where, terms):
    return pl.pallas_call(
        kernel,
        out_shape=[out((terms[0].shape[1], 128), bf16)] * N,
        in_specs=[SMEM] + [VMEM] * N,
        out_specs=[VMEM] * N,
        compiler_params=params(6),
        name=name,
    )(where, *terms)


def scatter(blocks, axes):
    return [blocks[0]] + [shift(blocks[by], axes, (by, by)) for by in (1, 2, 3)]


def moment_kernel(
    where, a0, a1, a2, a3, c0, c1, c2, c3, qm, theirs, km, qm_out, km_out, gram0, gram1, peak
):
    core = where[3]
    part = total(a0[...], a1[...], a2[...], a3[...])
    rows = pl.ds(0, MC)
    part_c = total(c0[rows, :], c1[rows, :], c2[rows, :], c3[rows, :])
    rows = pl.ds(MC, ML)
    value = join_logits(c0[rows, :])
    for ref in (c1, c2, c3):
        value = jnp.maximum(value, join_logits(ref[rows, :]))
    peak[...] = jnp.broadcast_to(value, (8, 128))
    for lane in range(3):
        lanes = pl.ds(lane * 128, 128)
        for owner in range(2):
            rows = pl.ds(owner * RP, RP)
            start = owner * MP + lane * RP
            moment = jnp.where(core == owner, qm[rows, lanes], theirs[:, lanes])
            qm_out[rows, lanes] = momentum_decay * moment + part[start : start + RP]
        rows = pl.ds(2 * RP, RC)
        qm_out[rows, lanes] = (
            momentum_decay * qm[rows, lanes] + part_c[lane * RC : (lane + 1) * RC]
        )
    for lane in range(2):
        lanes = pl.ds(lane * 128, 128)
        start = 3 * RC + lane * KR
        km_out[:, lanes] = momentum_decay * km[:, lanes] + part_c[start : start + KR]

    def gram_of(value):
        return lax.dot_general(
            value, value, (((0,), (0,)), ((), ())), precision=HIGHEST, preferred_element_type=f32
        )

    full = qm_out[...]
    for head, to in enumerate((gram0, gram1)):
        wide = (full if head == 0 else pltpu.roll(full, QH, 1))[:, :256]
        gram = gram_of(wide)
        left = lax.broadcasted_iota(jnp.int32, (64, 128), 1) < 64
        to[pl.ds(0, 64), :] = jnp.where(
            left, gram[:64, :128], pltpu.roll(gram[128:192, 128:], 64, 1)
        )
        to[pl.ds(64, 128), :] = gram[64:192, :128]
        gram = gram_of(km_out[:, pl.ds(head * KH, KH)])
        to[pl.ds(192, 64), :] = gram[64:]
        to[pl.ds(256, 32), :] = jnp.where(left[:32], gram[:32], pltpu.roll(gram[32:64], 64, 1))


def moments(where, part, part_c, query_moment, theirs, key_moment):
    return pl.pallas_call(
        moment_kernel,
        out_shape=(
            out((QR, QC), f32),
            out((KR, KC), f32),
            out((G_ROWS, 128), f32),
            out((G_ROWS, 128), f32),
            out((8, 128), f32),
        ),
        in_specs=[SMEM] + [VMEM] * 11,
        out_specs=(VMEM,) * 5,
        compiler_params=params(12),
        name="moments",
    )(where, *part, *part_c, query_moment, theirs, key_moment)


def three_products(left, right):
    def halves(value):
        high = value.astype(bf16)
        return high, (value - high.astype(f32)).astype(bf16)

    def product(first, second):
        return jnp.dot(first, second, preferred_element_type=f32)

    (left_high, left_low), (right_high, right_low) = halves(left), halves(right)
    return product(left_high, right_high) + (
        product(left_high, right_low) + product(left_low, right_high)
    )


def chain_kernel(g0, g1, g2, g3, to):
    packed = g0[...] + g1[...] + g2[...] + g3[...]
    row = lax.broadcasted_iota(jnp.int32, (256, 256), 0)
    column = lax.broadcasted_iota(jnp.int32, (256, 256), 1)
    left = lax.broadcasted_iota(jnp.int32, (64, 128), 1) < 64
    zeros = jnp.zeros((64, 128), f32)

    def stacked(*blocks):
        return jnp.concatenate(blocks, axis=0)

    def part(block, keep_left):
        return jnp.where(left if keep_left else ~left, block, 0.0)

    diagonal, middle, last = packed[:64], packed[64:128], packed[128:192]
    lower = stacked(zeros, part(middle, True), last, zeros)
    first = lower + stacked(part(diagonal, True), part(middle, False), zeros, zeros)
    corner = part(pltpu.roll(diagonal, 64, 1), True)
    query_gram = jnp.concatenate(
        [first, stacked(zeros, zeros, corner, zeros)], axis=1
    ) + stacked(lower.T, jnp.zeros((128, 256), f32))
    middle, diagonal = packed[192:256], packed[256:288]
    lower = stacked(zeros, part(middle, True))
    diagonal = part(stacked(diagonal, pltpu.roll(diagonal, 64, 1)), True)
    key_gram = lower + lower.T + stacked(diagonal, part(middle, False))
    query_eye = jnp.where((row == column) & (row < QH), 1.0, 0.0).astype(f32)
    key_eye = jnp.where(row == column, 1.0, 0.0).astype(f32)[:128, :128]

    def product(left, right, exact):
        if left.shape[0] < left.shape[1]:
            right = stacked(right, zeros_wide)
        if exact:
            return jnp.dot(left, right, precision=HIGHEST, preferred_element_type=f32)
        return three_products(left, right)

    zeros_wide = jnp.zeros((64, 256), f32)
    query_gram, query_eye = query_gram[:QH], query_eye[:QH]

    def start(gram, eye):
        square = jnp.sum(jnp.sum(gram * eye, axis=1, keepdims=True), axis=0, keepdims=True)
        inverse = 1.0 / (jnp.sqrt(square) + norm_epsilon)
        return gram * inverse * inverse, inverse

    grams, inverses = zip(start(query_gram, query_eye), start(key_gram, key_eye))
    grams, eyes, totals = list(grams), (query_eye, key_eye), [None, None]
    for iteration in range(ITERS):
        exact = iteration < 2
        mixers = []
        for i in range(2):
            square = product(grams[i], grams[i], exact)
            mixers.append(coef_first * eyes[i] + coef_second * grams[i] + coef_third * square)
        if iteration < ITERS - 1:
            halves = [product(mixers[i], grams[i], exact) for i in range(2)]
        for i in range(2):
            totals[i] = mixers[i] if iteration == 0 else product(totals[i], mixers[i], exact)
        if iteration < ITERS - 1:
            grams = [product(halves[i], mixers[i], exact) for i in range(2)]
    query_total, key_total = (totals[i] * inverses[i] for i in range(2))
    to[pl.ds(0, 192), :] = query_total[:192, :128]
    to[pl.ds(192, 192), :] = query_total[:192, 128:]
    to[pl.ds(384, 128), :] = key_total


def chain(grams):
    return pl.pallas_call(
        chain_kernel,
        out_shape=out((512, 128), f32),
        in_specs=[VMEM] * 4,
        out_specs=VMEM,
        compiler_params=params(12),
        name="newton_schulz_polynomial",
    )(*grams)

def update_kernel(where, own, other, peak, qm, km, qw, kw, to):
    z, x, _, core = read(where)
    mine, theirs = own[...], other[...]
    packs = (jnp.where(core == 0, mine, theirs), jnp.where(core == 0, theirs, mine))

    product = three_products
    gamma = jnp.minimum(1.0, clip_limit / peak[pl.ds(0, 1), :])
    lane = lax.broadcasted_iota(jnp.int32, (1, 128), 1)
    first_head = 2 * (z * N + x)
    gammas = [
        jnp.sum(jnp.where(lane == first_head + h, gamma, 0.0), axis=1, keepdims=True)
        for h in range(2)
    ]
    roots = [jnp.sqrt(g) for g in gammas]
    column = lax.broadcasted_iota(jnp.int32, (1, QC), 1)
    second = column >= QH
    rope = jnp.where(second, column - QH, column) >= QH - QROPE
    query_factor = jnp.where(
        rope, jnp.where(second, gammas[1], gammas[0]), jnp.where(second, roots[1], roots[0])
    )
    key_factor = jnp.where(
        lax.broadcasted_iota(jnp.int32, (1, KC), 1) >= KH, roots[1], roots[0]
    )

    full = qm[...]
    zeros = jnp.zeros((64, 256), f32)
    pad = jnp.zeros((QR, 128), f32)
    pieces = []
    for head in range(2):
        wide = (full if head == 0 else pltpu.roll(full, QH, 1))[:, :256]
        matrix = jnp.concatenate([packs[head][:192], packs[head][192:384]], axis=1)
        matrix = jnp.concatenate([matrix, zeros], axis=0)
        piece = jnp.concatenate([product(wide, matrix), pad], axis=1)
        pieces.append(piece if head == 0 else pltpu.roll(piece, QH, 1))
    query_ortho = pieces[0] + pieces[1]
    key_ortho = jnp.concatenate(
        [product(km[:, pl.ds(h * KH, KH)], packs[h][384:]) for h in range(2)], axis=1
    )
    query_scale = 0.2 * math.sqrt(max(QL, QH))
    key_scale = 0.2 * math.sqrt(max(KVL, KH))
    query_weight, key_weight = qw[...], kw[...]
    query_next = query_weight - learn_rate * (
        query_scale * query_ortho + weight_decay * query_weight
    )
    key_next = key_weight - learn_rate * (key_scale * key_ortho + weight_decay * key_weight)
    query_block = (query_next * query_factor).astype(bf16)
    key_block = (key_next * key_factor).astype(bf16)
    for lane in range(3):
        to[pl.ds(lane * QR, QR), :] = query_block[:, lane * 128 : (lane + 1) * 128]
    for lane in range(2):
        to[pl.ds(3 * QR + lane * KR, KR), :] = key_block[:, lane * 128 : (lane + 1) * 128]


def update(where, own, other, peak, query_moment, key_moment, query_weight, key_weight):
    return pl.pallas_call(
        update_kernel,
        out_shape=out((M_ALL, 128), bf16),
        in_specs=[SMEM] + [VMEM] * 7,
        out_specs=VMEM,
        compiler_params=params(12),
        name="update",
    )(where, own, other, peak, query_moment, key_moment, query_weight, key_weight)


def gathered_pieces(where, far, i, stack, query_out, key_out):
    z, x, _, core = read(where)
    for j in range(2):
        near = 2 * i + j
        back_z, back_x = jnp.where(core == 0, near, far), jnp.where(core == 0, far, near)
        zz, xx = (z + N - back_z) % N, (x + N - back_x) % N
        for lane in range(3):
            rows = pl.ds(lane * QR, QR)
            yield stack.at[j, rows, :], query_out.at[:, columns(zz, xx, QC, lane)]
        for lane in range(2):
            rows = pl.ds(3 * QR + lane * KR, KR)
            yield stack.at[j, rows, :], key_out.at[:, columns(zz, xx, KC, lane)]


def assemble_kernel(where, f0, f1, f3, s0, s1, s3, s2, query_out, key_out):
    for i, stacks in enumerate(((f0, f1, f3), (s0, s1, s3, s2))):
        for far, stack in zip((0, 1, 3, 2), stacks):
            for source, to in gathered_pieces(where, far, i, stack, query_out, key_out):
                to[...] = source[...]


RESULT = (pltpu.HBM((QR, N * N * QC), bf16), pltpu.HBM((KR, N * N * KC), bf16))


def assemble(where, first, second):
    return pl.pallas_call(
        assemble_kernel,
        out_shape=RESULT,
        in_specs=[SMEM] + [VMEM] * 7,
        out_specs=(VMEM, VMEM),
        compiler_params=params(16),
        name="assemble",
    )(where, *first, *second)


def finish_kernel(where, query_in, key_in, first, query_out, key_out, sems):
    copies = []
    for source, to in gathered_pieces(where, 2, 0, first, query_out, key_out):
        copies.append(pltpu.make_async_copy(source, to, sems.at[len(copies)]))
    for copy in copies:
        copy.start()
    for copy in copies:
        copy.wait()


def finish(where, query_out, key_out, first):
    return pl.pallas_call(
        finish_kernel,
        out_shape=RESULT,
        in_specs=[SMEM, HBM, HBM, VMEM],
        out_specs=(HBM, HBM),
        scratch_shapes=[pltpu.SemaphoreType.DMA((10,))],
        input_output_aliases={1: 0, 2: 1},
        compiler_params=params(4),
        name="finish",
    )(where, *in_hbm(query_out, key_out), first)


def on_device(grad_query, grad_key, query_weight, key_weight, query_moment, key_moment, max_logits):
    dp, ctx = lax.axis_index("dp"), lax.axis_index("ctx")
    z, x, y, core = dp // N, dp % N, ctx // 2, ctx % 2
    where = jnp.stack([z, x, y, core]).astype(jnp.int32)
    query = grad_query.reshape(N, 2, QR, N * N * QC)
    key = grad_key.reshape(N, 2, KR, N * N * KC)

    def after(value):
        return lax.optimization_barrier((where, value))[0]

    others, token = [], where
    for step in range(1, N):
        (blocks,) = local(None, step, token, query, key, max_logits)
        token = after(blocks)
        others.append(swap(blocks))
    pre = [local(1, None, where, query, key, max_logits, others[0])]
    *sums, blocks = local(2, N, after(pre[0][0]), query, key, max_logits, others[1])
    pre.append(sums)
    others.append(swap(blocks))
    for step in range(3, N + 1):
        pre.append(local(step, None, where, query, key, max_logits, others[step - 1]))

    p, m, c = pre[0]
    for step in range(1, N):
        p = shift(p, ("x", "z"), (1, 1))
        m = shift(m, ("x", "z"), (-1, -1))
        c = shift(c, ("y", "y"), (1, -1))
        if step < N - 1:
            p, m, c = add(pre[step][0], p), add(pre[step][1], m), add_c(pre[step][2], c)
        if step == 1:
            theirs = swap(lax.dynamic_slice_in_dim(query_moment, (1 - after(c)[3]) * RP, RP, 0))
    pre = pre[-1]

    part = split_ab(where, pre[:2], (p, m))
    part_c = split_c(after(part[0]), pre[2], c)
    part, part_c = scatter(part, ("y", "x")), scatter(part_c, ("z", "z"))
    part = next_parts(next_ab_kernel, "next_ab", where, part)
    part_c = next_parts(next_c_kernel, "next_c", after(part[0]), part_c)
    part, part_c = scatter(part, ("z", "y")), scatter(part_c, ("x", "x"))
    moment, new_key_moment, gram0, gram1, peak = moments(
        where, part, part_c, query_moment, theirs, key_moment
    )

    keep, give = jnp.where(core == 0, gram0, gram1), jnp.where(core == 0, gram1, gram0)
    gram = keep + swap(give)
    own = chain([gram] + [shift(gram, ("y", "y"), (by, by)) for by in (1, 2, 3)])

    theirs = swap(lax.dynamic_slice_in_dim(moment, (1 - core) * RP, RP, 0))
    new_query_moment = jnp.concatenate(
        [
            jnp.where(core == 0, moment[:RP], theirs),
            jnp.where(core == 0, theirs, moment[RP : 2 * RP]),
            moment[2 * RP :],
        ]
    )
    block = update(
        where, own, swap(own), peak, new_query_moment, new_key_moment, query_weight, key_weight
    )
    blocks = [block] + [shift(block, ("z", "x"), (by, by)) for by in (1, 2, 3)]

    def along(stack, by):
        return shift(stack, ("x", "z"), (by, by))

    first, second = jnp.stack(blocks[:2]), jnp.stack(blocks[2:])
    first_back, second_ahead = along(first, 1), along(second, -1)
    second_back, first_ahead = along(second, 1), along(first, -1)
    first_far, second_far = along(first_back, 1), along(second_ahead, -1)
    query_out, key_out = assemble(
        where, (first, first_back, first_ahead), (second, second_back, second_ahead, second_far)
    )
    query_out, key_out = finish(where, query_out, key_out, first_far)
    return (query_out, key_out, new_query_moment, new_key_moment)


def solution(mesh):
    in_specs = (
        P(("dp", "ctx"), None, None),
        P(("dp", "ctx"), None, None),
        P("ctx", "dp"),
        P("ctx", "dp"),
        P("ctx", "dp"),
        P("ctx", "dp"),
        P(("dp", "ctx"), None),
    )
    out_specs = (P("ctx", None), P("ctx", None), P("ctx", "dp"), P("ctx", "dp"))
    return jax.shard_map(
        on_device, mesh=mesh, in_specs=in_specs, out_specs=out_specs, check_vma=False
    )
```
